128 devices in a mesh: seq: 4 (over z_hi, core), dp: 32 (over y, z_lo, x).
Axes of the slice: x: 4, y: 4, z: 4 (z_hi: 2, z_lo: 2; z = z_hi * 2 + z_lo), core: 2. Of those that a mesh axis runs over, the one named last changes fastest.
Arguments:
- token_ids: int32 [32, 1024], P(None, 'seq'), may hold values from 0 to 50303
- doc_ids: int32 [32, 1024], P('dp'), may hold values from 0 to 1023, as said below
- pick_slots: int32 [32, 256], P(None, 'seq'), may hold values from -1 to 255, as said below
- labels: int32 [32, 256], P(None, 'seq'), may hold values from 0 to 50303
- vocab_table: float32 [25152, 1536], P('dp', 'seq'), may hold values from -0.4330127 to 0.4330127
- vocab_first: float32 [25152, 1536], P('dp', 'seq'), may hold values from -1.9073486e-06 to 1.9073486e-06
- vocab_second: float32 [25152, 1536], P('dp', 'seq'), may hold values from 7.463293e-15 to 2.985317e-14
- positions: float32 [1024, 768], P('seq'), may hold values from -0.625 to 0.625
- positions_first: float32 [1024, 768], P('seq'), may hold values from -1.9073486e-06 to 1.9073486e-06
- positions_second: float32 [1024, 768], P('seq'), may hold values from 7.463293e-15 to 2.985317e-14
- small_params: float32 [26, 768], replicated, may hold values from -0.4 to 1.3
- small_first: float32 [26, 768], replicated, may hold values from -9.536743e-06 to 9.536743e-06
- small_second: float32 [26, 768], replicated, may hold values from 1.8658232e-13 to 7.4632927e-13
- weights: float32 [384, 36864], P(('seq', 'dp')), may hold values from -0.14433757 to 0.14433757
- stat_left: float32 [384, 36864], P(('seq', 'dp')), may hold values from -3.181154e-11 to 6.680423e-10, as said below
- stat_right: float32 [384, 36864], P(('seq', 'dp')), may hold values from -3.181154e-11 to 6.680423e-10, as said below
- root_left: float32 [384, 36864], P(('seq', 'dp')), may hold values from -32.51477 to 563.17235, as said below
- root_right: float32 [384, 36864], P(('seq', 'dp')), may hold values from -32.51477 to 563.17235, as said below
- anchor: float32 [384, 36864], P(('seq', 'dp')), may hold values from -0.185334635 to 0.185334635
- fisher: float32 [384, 36864], P(('seq', 'dp')), may hold values from 4.6645576e-09 to 1.865823e-08
- owners: int32 [2, 192], replicated, may hold values from 0 to 191, as said below
Outputs:
- ce_sum: float32 [], replicated
- pick_count: float32 [], replicated
- grad_norm: float32 [], replicated
- vocab_new: float32 [25152, 1536], P('dp', 'seq')
- vocab_first_new: float32 [25152, 1536], P('dp', 'seq')
- vocab_second_new: float32 [25152, 1536], P('dp', 'seq')
- positions_new: float32 [1024, 768], P('seq')
- positions_first_new: float32 [1024, 768], P('seq')
- positions_second_new: float32 [1024, 768], P('seq')
- small_new: float32 [26, 768], replicated
- small_first_new: float32 [26, 768], replicated
- small_second_new: float32 [26, 768], replicated
- weights_new: float32 [384, 36864], P(('seq', 'dp'))
- stat_left_new: float32 [384, 36864], P(('seq', 'dp'))
- stat_right_new: float32 [384, 36864], P(('seq', 'dp'))
- block_grad: float32 [384, 36864], P(('seq', 'dp'))
- fisher_new: float32 [384, 36864], P(('seq', 'dp'))
The draws below stay inside these ranges and needn't reach their ends.
Inputs may be any that keep to these rules, and one draw needn't show every extreme that they name: `doc_ids`: each row starts at 0 and never falls; a document's number is the position of its first token; in each row one document covers all positions from one below 256 to one at or past 1024 - 256, and the last position is a document of its own. `pick_slots`: columns s * 64 to (s + 1) * 64 - 1 of a row hold distinct offsets into positions s * 256 to (s + 1) * 256 - 1 of that sequence, or -1; the last row's last 64 columns hold no -1. `owners`: each row is a permutation. `stat_left`: each block symmetric. `stat_right`: each block symmetric. `root_left`: each block symmetric. `root_right`: each block symmetric.
All inputs are finite; a program needn't handle non-finite values.
Results may differ from the reference program's by a relative error of at most 0.004.
The reference program's roundings to bfloat16 on the way count: a program that leaves them out, or rounds other values in their place, can miss the bound.
Values may be sent and summed in bfloat16 or wider, within the bound.
No kernel may reach another device: no remote copies, remote signals or barrier semaphores. Data moves between devices by JAX's collectives and lax.ppermute only.
A program may use at most 448 MiB of HBM per device.

```python
import math
import jax
import jax.numpy as jnp
import numpy as np
from jax import lax

D = 768
HEADS = 12
HEAD_DIM = 64
FF = 3072
VOCAB = 50304
LAYERS = 2
BS = 192
STEP = 10
PICK_DEV = 64
LOCAL_LEN = 256
LEN = 1024
ROWS = 32
PICKS = 256
NBLK = 384
BPL = 192
SMALL = 26
NPARAM = 53595648


def owner_table(key):
    row_keys = jax.random.split(jax.random.fold_in(key, 101), LAYERS)
    return jax.vmap(lambda single: jax.random.permutation(single, BPL))(row_keys).astype(jnp.int32)


def slot_scale(key):
    table_ids = owner_table(key)
    unit = D // BS
    fc_end = 4 * unit * unit + unit * (FF // BS)
    scale = jnp.where(table_ids < fc_end, D ** (-0.5), 0.25 * FF ** (-0.5)).astype(jnp.float32)
    return scale.reshape(NBLK, 1)


def normal_noise(key, shape):
    return jnp.clip(jax.random.normal(key, shape, jnp.float32), -4.0, 4.0)


def stat_matrix(diag_factor, noise, scale, offdiag):
    eye_mat = jnp.eye(BS, dtype=jnp.float32)
    mirrored = 0.5 * (noise + jnp.swapaxes(noise, 1, 2))
    full = scale * (eye_mat * diag_factor[:, :, None] + offdiag * mirrored * (1.0 - eye_mat))
    return full.reshape(NBLK, BS * BS)


def draw_owners(key, part):
    return owner_table(key)


def draw_weights(key, part):
    scale = slot_scale(key)
    noise_key = jax.random.fold_in(key, 1)
    noise = normal_noise(noise_key, (NBLK, BS * BS))
    return noise * scale


def draw_anchor(key, part):
    scale = slot_scale(key)
    noise_key = jax.random.fold_in(key, 1)
    noise = normal_noise(noise_key, (NBLK, BS * BS))
    key = jax.random.fold_in(key, 2)
    offset = 1.4 * NPARAM ** 0.5 / 1000000.0
    return noise * scale + offset * normal_noise(key, (NBLK, BS * BS))


def draw_stat_left(key, part):
    key = jax.random.fold_in(key, 3)
    diag_key, noise_key = jax.random.split(key)
    factor = jnp.exp(jax.random.uniform(diag_key, (NBLK, BS), jnp.float32, 0.0, 1.3862944))
    noise = normal_noise(noise_key, (NBLK, BS, BS))
    return stat_matrix(factor, noise, 4.44e-05 * BS / NPARAM, 0.05)


def draw_stat_right(key, part):
    key = jax.random.fold_in(key, 4)
    diag_key, noise_key = jax.random.split(key)
    factor = jnp.exp(jax.random.uniform(diag_key, (NBLK, BS), jnp.float32, 0.0, 1.3862944))
    noise = normal_noise(noise_key, (NBLK, BS, BS))
    return stat_matrix(factor, noise, 4.44e-05 * BS / NPARAM, 0.05)


def draw_root_left(key, part):
    key = jax.random.fold_in(key, 5)
    diag_key, noise_key = jax.random.split(key)
    factor = jax.random.uniform(diag_key, (NBLK, BS), jnp.float32, 1.0, 2.0)
    noise = normal_noise(noise_key, (NBLK, BS, BS))
    return stat_matrix(factor, noise, (4.44e-05 * BS / NPARAM) ** (-0.25), 0.4 * BS ** (-0.5))


def draw_root_right(key, part):
    key = jax.random.fold_in(key, 6)
    diag_key, noise_key = jax.random.split(key)
    factor = jax.random.uniform(diag_key, (NBLK, BS), jnp.float32, 1.0, 2.0)
    noise = normal_noise(noise_key, (NBLK, BS, BS))
    return stat_matrix(factor, noise, (4.44e-05 * BS / NPARAM) ** (-0.25), 0.4 * BS ** (-0.5))


def draw_vocab_table(key, part):
    key = jax.random.fold_in(key, 7)
    rank = (jnp.arange(VOCAB, dtype=jnp.float32) / (VOCAB - 1))[:, None]
    noise = normal_noise(key, (VOCAB, D))
    rise = 2.0
    return (noise * (1.0 + rise * rank) * D ** (-0.5)).reshape(VOCAB // 2, 2 * D)


def draw_small_params(key, part):
    key = jax.random.fold_in(key, 8)
    gain_key, noise_key = jax.random.split(key)
    row_index = jnp.arange(SMALL)[:, None]
    gains = 1.0 + jax.random.uniform(gain_key, (SMALL, D), jnp.float32, -0.3, 0.3)
    rest = 0.1 * normal_noise(noise_key, (SMALL, D))
    return jnp.where(row_index < 2 * LAYERS + 1, gains, rest)


def draw_doc_ids(key, part):
    key = jax.random.fold_in(key, 9)
    start_key, stop_key, flag_key = jax.random.split(key, 3)
    places = jnp.arange(LEN)[None, :]
    start_at = jax.random.randint(start_key, (ROWS, 1), 0, LOCAL_LEN)
    stop_at = jax.random.randint(stop_key, (ROWS, 1), LEN - LOCAL_LEN, LEN - 1)
    flags = (jax.random.randint(flag_key, (ROWS, LEN), 0, 48) == 0).astype(jnp.int32)
    flags = jnp.where((places > start_at) & (places <= stop_at), 0, flags)
    flags = jnp.where((places == start_at) | (places == stop_at + 1) | (places == LEN - 1), 1, flags)
    flags = jnp.where(places == 0, 0, flags)
    starts = jnp.where(flags == 1, places, 0).astype(jnp.int32)
    return lax.cummax(starts, axis=1).astype(jnp.int32)


def draw_pick_slots(key, part):
    key = jax.random.fold_in(key, 10)
    perm_key, use_key = jax.random.split(key)
    blocks = LEN // LOCAL_LEN
    block_keys = jax.random.split(perm_key, ROWS * blocks)
    offsets = jax.vmap(lambda single: jax.random.permutation(single, LOCAL_LEN)[:PICK_DEV])(block_keys)
    offsets = offsets.reshape(ROWS, blocks, PICK_DEV)
    row_index = jnp.arange(ROWS)[:, None, None]
    block_index = jnp.arange(blocks)[None, :, None]
    limit = (ROWS - 1) * (blocks - 1) + row_index * (blocks - 1) + block_index * (ROWS - 1)
    chance = jax.random.randint(use_key, (ROWS, blocks, PICK_DEV), 0, 3 * (ROWS - 1) * (blocks - 1))
    return jnp.where(chance < limit, offsets, -1).reshape(ROWS, blocks * PICK_DEV).astype(jnp.int32)


def place_ends(entries, rng, low, top_value):
    index_at = [jax.random.randint(jax.random.fold_in(rng, axis), (), 0, length) for axis, length in enumerate(entries.shape)]
    widest = entries.shape.index(max(entries.shape))
    neighbour = index_at[:widest] + [(index_at[widest] + 1) % entries.shape[widest]] + index_at[widest + 1:]
    return entries.at[tuple(index_at)].set(low).at[tuple(neighbour)].set(top_value)


def block_levels(key, dims, cuts, low, largest):
    factor_of, own = 1.0, jax.random.fold_in(key, 6)
    for position, parts in cuts:
        steps = jnp.exp(jax.random.uniform(jax.random.fold_in(own, position), (parts,), jnp.float32, low / len(cuts), largest / len(cuts)))
        factor_of = factor_of * jnp.repeat(steps, dims[position] // parts).reshape([-1 if axis == position else 1 for axis in range(len(dims))])
    return factor_of


def cumulative_ranks(number_of, skew):
    weights = [(1 << 20) // math.isqrt(rank ** skew) + 1 for rank in range(1, number_of + 1)]
    width = 1 + sum(weights) // (1 << 30)
    return np.cumsum(np.array([max(1, weight // width) for weight in weights]))


def ranked_ids(own_key, dims, number_of, skew):
    table = cumulative_ranks(number_of, skew)
    lot = jax.random.randint(jax.random.fold_in(own_key, 1), dims, 0, int(table[number_of - 1]))
    grade = jnp.searchsorted(jnp.asarray(table, jnp.int32), lot, side="right")
    return jax.random.permutation(jax.random.fold_in(own_key, 2), number_of)[grade].astype(jnp.int32)


def bell_draw(key, dims, width, most, cuts=(), kind=jnp.bfloat16):
    entries = width * jax.random.normal(key, dims, jnp.float32)
    if cuts:
        entries = entries * block_levels(key, dims, cuts, -0.22, 0.18)
    return jnp.clip(entries, -most, most).astype(kind)


def setup_inputs(seed: int = 0) -> dict:
    key_of = jax.random.split(jax.random.key(seed), 22)
    return {
        "token_ids": place_ends(ranked_ids(key_of[0], (ROWS, LEN), VOCAB, 2), jax.random.fold_in(key_of[0], 3), 0, VOCAB - 1).astype(jnp.int32),
        "doc_ids": draw_doc_ids(jax.random.fold_in(key_of[21], 71), 0),
        "pick_slots": draw_pick_slots(jax.random.fold_in(key_of[21], 71), 0),
        "labels": place_ends(ranked_ids(key_of[3], (ROWS, PICKS), VOCAB, 2), jax.random.fold_in(key_of[3], 3), 0, VOCAB - 1).astype(jnp.int32),
        "vocab_table": draw_vocab_table(jax.random.fold_in(key_of[21], 71), 0),
        "vocab_first": bell_draw(key_of[5], (VOCAB // 2, 2 * D), (0.00222 / NPARAM ** 0.5), 1.9073486328125e-06, ((0, 32), (1, 4)), jnp.float32),
        "vocab_second": jnp.clip(jnp.exp(math.log(2.985317139434125e-14) - 1.3862944 * jax.random.uniform(key_of[6], (VOCAB // 2, 2 * D), jnp.float32) ** block_levels(key_of[6], (VOCAB // 2, 2 * D), ((0, 32), (1, 4)), -0.2, 0.2)), 7.463292848585313e-15, 2.985317139434125e-14),
        "positions": bell_draw(key_of[7], (LEN, D), 0.1, 0.625, ((0, 4),), jnp.float32),
        "positions_first": bell_draw(key_of[8], (LEN, D), (0.00222 / NPARAM ** 0.5), 1.9073486328125e-06, ((0, 4),), jnp.float32),
        "positions_second": jnp.clip(jnp.exp(math.log(2.985317139434125e-14) - 1.3862944 * jax.random.uniform(key_of[9], (LEN, D), jnp.float32) ** block_levels(key_of[9], (LEN, D), ((0, 4),), -0.2, 0.2)), 7.463292848585313e-15, 2.985317139434125e-14),
        "small_params": draw_small_params(jax.random.fold_in(key_of[21], 71), 0),
        "small_first": bell_draw(key_of[11], (SMALL, D), (0.0111 / NPARAM ** 0.5), 9.5367431640625e-06, (), jnp.float32),
        "small_second": jnp.clip(jnp.exp(jax.random.uniform(key_of[12], (SMALL, D), jnp.float32, math.log(1.865823169794681e-13), math.log(7.463292679178724e-13))), 1.865823169794681e-13, 7.463292679178724e-13),
        "weights": draw_weights(jax.random.fold_in(key_of[21], 71), 0),
        "stat_left": draw_stat_left(jax.random.fold_in(key_of[21], 71), 0),
        "stat_right": draw_stat_right(jax.random.fold_in(key_of[21], 71), 0),
        "root_left": draw_root_left(jax.random.fold_in(key_of[21], 71), 0),
        "root_right": draw_root_right(jax.random.fold_in(key_of[21], 71), 0),
        "anchor": draw_anchor(jax.random.fold_in(key_of[21], 71), 0),
        "fisher": jnp.clip(jnp.exp(math.log(1.865823051616644e-08) - 1.3862944 * jax.random.uniform(key_of[19], (NBLK, BS * BS), jnp.float32) ** block_levels(key_of[19], (NBLK, BS * BS), ((0, 128),), -0.2, 0.2)), 4.66455762904161e-09, 1.865823051616644e-08),
        "owners": draw_owners(jax.random.fold_in(key_of[21], 71), 0),
    }


exact_prec = lax.Precision.HIGHEST
clip_bound = 0.02
ewc_weight = 1000000.0
fisher_decay = 0.8
first_decay = 0.9
second_decay = 0.999
adam_epsilon = 1e-08
table_rate = 0.05
small_rate = 0.1
decay_rate = 0.1
stat_decay = 0.9
shampoo_rate = 0.02
graft_epsilon = 1e-06

@jax.custom_vjp
def low(v):
    return lax.optimization_barrier(v.astype(jnp.bfloat16)).astype(jnp.float32)

@jax.custom_vjp
def low_back(v):
    return v

def low_keep(v):
    return (low(v), None)

def low_pass(kept, grad):
    return (grad,)

def back_keep(v):
    return (v, None)

def back_low(kept, grad):
    return (low(grad),)
low.defvjp(low_keep, low_pass)
low_back.defvjp(back_keep, back_low)

def matmul(left, right):
    return jnp.dot(left, right, precision=exact_prec, preferred_element_type=jnp.float32)

def layer_norm(values_in, gain, shift):
    centre = lax.optimization_barrier(jnp.mean(values_in, axis=-1, keepdims=True))
    cent = values_in - centre
    spread = lax.optimization_barrier(jnp.mean(cent * cent, axis=-1, keepdims=True))
    return cent * lax.rsqrt(spread + 1e-05) * gain + shift

def assemble(blocks, row_count, col_count):
    tile_size = blocks.shape[-1]
    grid = blocks.reshape(row_count, col_count, tile_size, tile_size).transpose(0, 2, 1, 3)
    return grid.reshape(row_count * tile_size, col_count * tile_size)

def layer_mats(natural):
    unit = D // BS
    wide = FF // BS
    first_end = 3 * unit * unit
    second_end = first_end + unit * unit
    third_end = second_end + unit * wide
    return (assemble(natural[:first_end], unit, 3 * unit), assemble(natural[first_end:second_end], unit, unit), assemble(natural[second_end:third_end], unit, wide), assemble(natural[third_end:], wide, unit))

def sequence_loss(table_f, positions, small_params, weights, owners, token_row, doc_row, pick_row, label_row):
    table_bf = low(table_f.reshape(VOCAB, D))
    tiles = low(weights.reshape(NBLK, BS, BS))
    inverse = jnp.argsort(owners, axis=1)
    residual = low_back(table_bf[token_row]) + positions
    places = jnp.arange(LEN)
    doc_mask = (places[:, None] >= places[None, :]) & (doc_row[:, None] == doc_row[None, :])
    gain_rows = 2 * LAYERS + 1
    for layer_idx in range(LAYERS):
        natural = tiles[layer_idx * BPL:(layer_idx + 1) * BPL][inverse[layer_idx]]
        w_qkv, w_proj, w_fc, w_out = layer_mats(natural)
        base_row = 2 * gain_rows + 8 * layer_idx
        bias_qkv = jnp.concatenate([small_params[base_row], jnp.zeros((D,), jnp.float32), small_params[base_row + 1]])
        normed = low(layer_norm(residual, small_params[2 * layer_idx], small_params[gain_rows + 2 * layer_idx]))
        qkv_all = low(low_back(matmul(normed, w_qkv) + bias_qkv))
        queries = qkv_all[:, :D].reshape(LEN, HEADS, HEAD_DIM)
        key_heads = qkv_all[:, D:2 * D].reshape(LEN, HEADS, HEAD_DIM)
        values = qkv_all[:, 2 * D:].reshape(LEN, HEADS, HEAD_DIM)
        scores = low_back(jnp.einsum('qhd,khd->hqk', queries, key_heads, precision=exact_prec) * 0.125)
        soft_probs = jax.nn.softmax(jnp.where(doc_mask[None], scores, -1e+30), axis=-1)
        attended = jnp.einsum('hqk,khd->qhd', low(soft_probs), values, precision=exact_prec).reshape(LEN, D)
        attended = low(low_back(attended))
        residual = residual + low_back(matmul(attended, w_proj) + small_params[base_row + 2])
        normed_b = low(layer_norm(residual, small_params[2 * layer_idx + 1], small_params[gain_rows + 2 * layer_idx + 1]))
        inner_pre = low_back(matmul(normed_b, w_fc) + small_params[base_row + 3:base_row + 7].reshape(FF))
        activated = low(jax.nn.gelu(inner_pre, approximate=True))
        residual = residual + low_back(matmul(activated, w_out) + small_params[base_row + 7])
    final_norm = low(layer_norm(residual, small_params[2 * LAYERS], small_params[gain_rows + 2 * LAYERS]))
    used = pick_row >= 0
    spots = jnp.arange(PICKS) // PICK_DEV * LOCAL_LEN + jnp.maximum(pick_row, 0)
    logits = low_back(jnp.dot(final_norm[spots], table_bf.T, precision=exact_prec))
    spread = jax.nn.logsumexp(logits, axis=-1)
    target = jnp.take_along_axis(logits, label_row[:, None], axis=1)[:, 0]
    return jnp.sum(jnp.where(used, spread - target, 0.0))

def adam_update(param, grad, first, second, rate, decay):
    first = first_decay * first + (1.0 - first_decay) * grad
    second = second_decay * second + (1.0 - second_decay) * grad * grad
    fixed_first = first / (1.0 - first_decay ** STEP)
    fixed_second = second / (1.0 - second_decay ** STEP)
    return (param - rate * (fixed_first / (jnp.sqrt(fixed_second) + adam_epsilon) + decay * param), first, second)

def shampoo(param, grad, left, right, root_l, root_r):
    left = stat_decay * left + (1.0 - stat_decay) * matmul(grad, grad.T)
    right = stat_decay * right + (1.0 - stat_decay) * matmul(grad.T, grad)
    direction = matmul(matmul(root_l, grad), root_r)
    direction = direction * lax.rsqrt(jnp.mean(direction * direction) + graft_epsilon)
    return (param - shampoo_rate * (direction + decay_rate * param), left, right)

def as_blocks(flat):
    return flat.reshape(NBLK, BS, BS)

def reference(token_ids, doc_ids, pick_slots, labels, vocab_table, vocab_first, vocab_second, positions, positions_first, positions_second, small_params, small_first, small_second, weights, stat_left, stat_right, root_left, root_right, anchor, fisher, owners):

    def one_row(carry, row_data):
        token_row, doc_row, pick_row, label_row = row_data
        value, back = jax.vjp(lambda ta, po, sm, we: sequence_loss(ta, po, sm, we, owners, token_row, doc_row, pick_row, label_row), vocab_table, positions, small_params, weights)
        grads = back(jnp.ones((), jnp.float32))
        return ((carry[0] + value, jax.tree.map(jnp.add, carry[1], grads)), None)
    zeros = (jnp.zeros_like(vocab_table), jnp.zeros_like(positions), jnp.zeros_like(small_params), jnp.zeros_like(weights))
    (ce_sum, grads), _ = lax.scan(one_row, (jnp.zeros((), jnp.float32), zeros), (token_ids, doc_ids, pick_slots, labels))
    pick_count = jnp.sum((pick_slots >= 0).astype(jnp.float32))
    g_table, g_pos, g_small, g_ce = [g / pick_count for g in grads]
    _, penalty_back = jax.vjp(lambda we: 0.5 * ewc_weight * jnp.sum(fisher * (we - anchor) ** 2), weights)
    g_blocks = g_ce + penalty_back(jnp.ones((), jnp.float32))[0]
    grad_norm = jnp.sqrt(jnp.sum(g_table * g_table) + jnp.sum(g_pos * g_pos) + jnp.sum(g_small * g_small) + jnp.sum(g_blocks * g_blocks))
    factor = jnp.minimum(1.0, clip_bound / grad_norm)
    table_new, table_first, table_second = adam_update(vocab_table, factor * g_table, vocab_first, vocab_second, table_rate, decay_rate)
    pos_new, pos_first, pos_second = adam_update(positions, factor * g_pos, positions_first, positions_second, table_rate, 0.0)
    small_new, small_first_new, small_second_new = adam_update(small_params, factor * g_small, small_first, small_second, small_rate, 0.0)
    block_grad = factor * g_blocks
    weights_new, left_new, right_new = jax.vmap(shampoo)(as_blocks(weights), as_blocks(block_grad), as_blocks(stat_left), as_blocks(stat_right), as_blocks(root_left), as_blocks(root_right))
    fisher_new = fisher_decay * fisher + (1.0 - fisher_decay) * g_ce * g_ce
    return (ce_sum, pick_count, grad_norm, table_new, table_first, table_second, pos_new, pos_first, pos_second, small_new, small_first_new, small_second_new, weights_new.reshape(NBLK, BS * BS), left_new.reshape(NBLK, BS * BS), right_new.reshape(NBLK, BS * BS), block_grad, fisher_new)
```

```python
import functools

import jax
import jax.numpy as jnp
from jax import lax
from jax.experimental import pallas as pl
from jax.experimental.pallas import tpu as pltpu
from jax.sharding import PartitionSpec as P

HEADS = 12
HEAD_DIM = 64
LAYERS = 2
BS = 192
STEP = 10
PACK = 288
LANES = 128
HALF = 96

exact_prec = lax.Precision.HIGHEST
clip_bound = 0.02
ewc_weight = 1000000.0
fisher_decay = 0.8
first_decay = 0.9
second_decay = 0.999
adam_epsilon = 1e-08
table_rate = 0.05
small_rate = 0.1
decay_rate = 0.1
stat_decay = 0.9
shampoo_rate = 0.02
graft_epsilon = 1e-06

BF = jnp.bfloat16
F32 = jnp.float32


def line(zh, c, y, zl, x):
    return (zh * 2 + c) * 32 + y * 8 + zl * 4 + x


def moved(axis, step, zh, c, y, zl, x):
    z = zh * 2 + zl
    if axis == "x":
        x = step(x, c)
    elif axis == "y":
        y = step(y, c)
    elif axis == "z":
        z = step(z, c)
        zh, zl = z // 2, z % 2
    elif axis == "c":
        c = 1 - c
    elif axis == "zl":
        zl = 1 - zl
    elif axis == "zh":
        zh = 1 - zh
    return zh, c, y, zl, x


COORDS = [
    (zh, c, y, zl, x)
    for zh in range(2)
    for c in range(2)
    for y in range(4)
    for zl in range(2)
    for x in range(4)
]


def permuted(value, axis, step, keep=None):
    pairs = [
        (line(*at), line(*moved(axis, step, *at))) for at in COORDS if keep is None or keep(*at)
    ]
    return lax.ppermute(value, ("seq", "dp"), pairs)


def turn(value, axis, amount):
    return permuted(value, axis, lambda at, c: (at + (amount if c == 0 else -amount)) % 4)


def swap(value, axis):
    return permuted(value, axis, None)


def crossed(value, axis, mask):
    return permuted(value, axis, lambda at, c: at ^ mask)


def z_flip(value):
    return turn(turn(value, "z", 1), "z", 1)


def gather4(value, axis):
    near = turn(value, axis, -1)
    other = turn(value, axis, 1)
    return [value, near, turn(near, axis, -1), other]


def gather4_direct(value, axis):
    return [value, turn(value, axis, -1), turn(value, axis, 2), turn(value, axis, 1)]


def wide(value):
    return value.astype(F32)


def reduce4(parts, axis, kind):
    first = turn(parts[2].astype(kind), axis, 1)
    onward = (wide(parts[1]) + wide(first)).astype(kind)
    near = turn(onward, axis, 1)
    other = turn(parts[3].astype(kind), axis, -1)
    return wide(parts[0]) + wide(near) + wide(other)


def reduce4_direct(parts, axis, kind):
    near = turn(parts[1].astype(kind), axis, 1)
    far = turn(parts[2].astype(kind), axis, 2)
    other = turn(parts[3].astype(kind), axis, -1)
    return wide(parts[0]) + wide(near) + wide(far) + wide(other)


def sum_everywhere(value):
    value = value + swap(value, "c")
    for axis in ("z", "y", "x"):
        one, two, three = (crossed(value, axis, mask) for mask in (1, 2, 3))
        value = (value + one) + (two + three)
    return value


def pack_blocks(blocks, odd):
    odd = odd[:, None, None]
    main = jnp.where(odd, blocks[:, :, BS - LANES :], blocks[:, :, :LANES])
    half = jnp.where(odd, blocks[:, :, : BS - LANES], blocks[:, :, LANES:])
    top, low = half[:, :HALF], half[:, HALF:]
    rest = jnp.concatenate([jnp.where(odd, low, top), jnp.where(odd, top, low)], axis=2)
    return jnp.concatenate([main, rest], axis=1)


def unpack_blocks(packed, odd):
    odd = odd[:, None, None]
    main, rest = packed[:, :BS], packed[:, BS:]
    left, right = rest[:, :, : LANES // 2], rest[:, :, LANES // 2 :]
    half = jnp.concatenate([jnp.where(odd, right, left), jnp.where(odd, left, right)], axis=1)
    return jnp.where(
        odd, jnp.concatenate([half, main], axis=2), jnp.concatenate([main, half], axis=2)
    )


def pieces_of(chunk):
    return (("y", 8, 4), ("x", 8, 4), ("zl", 16, 2))[chunk]


def inner_moves(chunk):
    if chunk == 0:
        return [(my, kz, mx) for my in range(4) for mx in range(4) for kz in range(2)]
    if chunk == 1:
        return [(my, kz, mx) for mx in range(4) for my in range(4) for kz in range(2)]
    return [(my, kz, mx) for kz in range(2) for my in range(4) for mx in range(4)]


MATRICES = ((0, 4, 12), (48, 4, 4), (64, 4, 16), (128, 16, 4))


def assemble_kernel(places, *refs):
    arrays, outs, (natural, sem) = refs[:20], refs[20:24], refs[24:]
    at = 0
    for array in arrays:
        count = array.shape[0]

        def fetch(q, carry, array=array, at=at):
            pltpu.make_async_copy(array.at[q], natural.at[places[at + q]], sem).start()
            return carry

        lax.fori_loop(0, count, fetch, 0)
        at += count
    pltpu.make_async_copy(natural, natural, sem).wait()
    left = lax.broadcasted_iota(jnp.int32, (HALF, LANES), 1) < LANES // 2
    for out, (base, tall, across) in zip(outs, MATRICES, strict=True):
        pairs = across // 2

        def place(t, carry, out=out, base=base, pairs=pairs):
            row = pl.multiple_of((t // pairs) * BS, HALF)
            col = pl.multiple_of((t % pairs) * 2 * BS, LANES)
            even, odd = base + 2 * t, base + 2 * t + 1
            out[pl.ds(row, BS), pl.ds(col, LANES)] = natural[even, :BS]
            out[pl.ds(row, BS), pl.ds(col + 2 * LANES, LANES)] = natural[odd, :BS]
            he, ho = wide(natural[even, BS:]), wide(natural[odd, BS:])
            out[pl.ds(row, HALF), pl.ds(col + LANES, LANES)] = jnp.where(left, he, ho).astype(BF)
            out[pl.ds(row + HALF, HALF), pl.ds(col + LANES, LANES)] = pltpu.roll(
                jnp.where(left, ho, he), LANES // 2, 1
            ).astype(BF)
            return carry

        lax.fori_loop(0, tall * pairs, place, 0)


def assemble_layer(places, arrays):
    shapes = [jax.ShapeDtypeStruct((t * BS, a * BS), BF) for _, t, a in MATRICES]
    return pl.pallas_call(
        assemble_kernel,
        grid_spec=pltpu.PrefetchScalarGridSpec(
            num_scalar_prefetch=1,
            grid=(),
            in_specs=[pl.BlockSpec(memory_space=pl.ANY)] * len(arrays),
            out_specs=[pl.BlockSpec(memory_space=pltpu.VMEM)] * 4,
            scratch_shapes=[pltpu.VMEM((BS, PACK, LANES), BF), pltpu.SemaphoreType.DMA],
        ),
        out_shape=shapes,
        compiler_params=pltpu.CompilerParams(vmem_limit_bytes=40 * 1024 * 1024),
        cost_estimate=pl.CostEstimate(flops=0, bytes_accessed=29_000_000, transcendentals=0),
        name="assemble",
    )(places, *arrays)


def weight_grad_kernel(places, *refs):
    lefts, rights, outs, (natural, sem) = refs[:4], refs[4:8], refs[8:14], refs[14:]
    left = lax.broadcasted_iota(jnp.int32, (HALF, LANES), 1) < LANES // 2
    for lhs, rhs, (base, tall, across) in zip(lefts, rights, MATRICES, strict=True):
        pairs = across // 2

        def unit(t, carry, lhs=lhs, rhs=rhs, base=base, across=across, pairs=pairs):
            rows, cols = t // pairs, t % pairs
            span = 2 * BS
            piece = lax.dot_general(
                lhs[:, pl.ds(pl.multiple_of(rows * span, LANES), span)],
                rhs[:, pl.ds(pl.multiple_of(cols * span, LANES), span)],
                (((0,), (0,)), ((), ())),
                preferred_element_type=F32,
            )
            for r in range(2):
                even = base + (2 * rows + r) * across + 2 * cols
                strip = piece[r * BS : (r + 1) * BS]
                natural[even, :BS] = strip[:, :LANES].astype(BF)
                natural[even + 1, :BS] = strip[:, 2 * LANES :].astype(BF)
                mid = strip[:, LANES : 2 * LANES]
                top = mid[:HALF]
                low = pltpu.roll(mid[HALF:], LANES // 2, 1)
                natural[even, BS:] = jnp.where(left, top, low).astype(BF)
                natural[even + 1, BS:] = jnp.where(left, low, top).astype(BF)
            return carry

        lax.fori_loop(0, (tall // 2) * pairs, unit, 0)
    at = 0
    for out in outs:

        def put(q, carry, out=out, at=at):
            pltpu.make_async_copy(natural.at[places[at + q]], out.at[q], sem).start()
            return carry

        lax.fori_loop(0, 32, put, 0)
        at += 32
    pltpu.make_async_copy(natural, natural, sem).wait()


def weight_grads(places, lefts, rights):
    return pl.pallas_call(
        weight_grad_kernel,
        grid_spec=pltpu.PrefetchScalarGridSpec(
            num_scalar_prefetch=1,
            grid=(),
            in_specs=[pl.BlockSpec(memory_space=pltpu.VMEM)] * 8,
            out_specs=[pl.BlockSpec(memory_space=pl.ANY)] * 6,
            scratch_shapes=[pltpu.VMEM((BS, PACK, LANES), BF), pltpu.SemaphoreType.DMA],
        ),
        out_shape=[jax.ShapeDtypeStruct((32, PACK, LANES), BF)] * 6,
        compiler_params=pltpu.CompilerParams(vmem_limit_bytes=40 * 1024 * 1024),
        cost_estimate=pl.CostEstimate(
            flops=2 * 256 * 7_077_888, bytes_accessed=21_000_000, transcendentals=0
        ),
        name="weight_grads",
    )(places, *lefts, *rights)


def lookup_kernel(ids, table, out0, out1, out2, out3):
    rows = table.shape[0]
    lane = lax.broadcasted_iota(jnp.int32, (ids.shape[0], LANES), 1)
    held = ids[...]
    hot = jnp.concatenate(
        [jnp.where(held == lane + at, 1.0, 0.0).astype(BF) for at in range(0, rows, LANES)], axis=1
    )
    found = jnp.dot(hot, table[...], preferred_element_type=F32).astype(BF)
    out0[...] = found[:, :256]
    out1[...] = found[:, 256:512]
    out2[...] = found[:256, 512:]
    out3[...] = found[256:, 512:]


def lookup(ids, table):
    tokens = ids.shape[0]
    steps = tokens // 512
    return pl.pallas_call(
        lookup_kernel,
        grid=(steps,),
        in_specs=[
            pl.BlockSpec((512, LANES), lambda t: (t, 0)),
            pl.BlockSpec(table.shape, lambda t: (0, 0)),
        ],
        out_specs=[
            pl.BlockSpec((512, 256), lambda t: (t, 0)),
            pl.BlockSpec((512, 256), lambda t: ((t % 4) * 4 + t // 4, 0)),
            pl.BlockSpec((256, 256), lambda t: (t, 0)),
            pl.BlockSpec((256, 256), lambda t: (t, 0)),
        ],
        out_shape=[
            jax.ShapeDtypeStruct((tokens, 256), BF),
            jax.ShapeDtypeStruct((tokens, 256), BF),
            jax.ShapeDtypeStruct((tokens // 2, 256), BF),
            jax.ShapeDtypeStruct((tokens // 2, 256), BF),
        ],
        compiler_params=pltpu.CompilerParams(vmem_limit_bytes=40 * 1024 * 1024),
        cost_estimate=pl.CostEstimate(
            flops=2 * tokens * table.shape[0] * 768, bytes_accessed=20_000_000, transcendentals=0
        ),
        name="lookup",
    )(ids, table)


def scatter_kernel(order, ids, start, part0, part1, part2, part3, out, sums):
    step = pl.program_id(0)

    @pl.when(step == 0)
    def _():
        out[...] = start[...]
        sums[...] = jnp.zeros(sums.shape, F32)

    rows, tokens = out.shape[0], ids.shape[2]
    place = lax.broadcasted_iota(jnp.int32, (rows, tokens), 0)
    hot = jnp.where(place == ids[0], 1.0, 0.0).astype(BF)
    last = jnp.concatenate([part2[...], part3[...]], axis=0)
    for at, part in enumerate((part0[...], part1[...], last)):
        cols = slice(at * 256, (at + 1) * 256)
        out[:, cols] += jnp.dot(hot, part, preferred_element_type=F32)
        sums[:, cols] += wide(part[:256]) + wide(part[256:])


def scatter_rows(order, ids, start, parts):
    return pl.pallas_call(
        scatter_kernel,
        grid_spec=pltpu.PrefetchScalarGridSpec(
            num_scalar_prefetch=1,
            grid=(16,),
            in_specs=[
                pl.BlockSpec((1, 1, 512), lambda t, order: (order[0, t], 0, 0)),
                pl.BlockSpec(start.shape, lambda t, order: (0, 0)),
                pl.BlockSpec((512, 256), lambda t, order: (order[0, t], 0)),
                pl.BlockSpec((512, 256), lambda t, order: (order[1, t], 0)),
                pl.BlockSpec((256, 256), lambda t, order: (order[0, t], 0)),
                pl.BlockSpec((256, 256), lambda t, order: (order[0, t], 0)),
            ],
            out_specs=[
                pl.BlockSpec(start.shape, lambda t, order: (0, 0)),
                pl.BlockSpec((256, 768), lambda t, order: (0, 0)),
            ],
        ),
        out_shape=[
            jax.ShapeDtypeStruct(start.shape, F32),
            jax.ShapeDtypeStruct((256, 768), F32),
        ],
        compiler_params=pltpu.CompilerParams(vmem_limit_bytes=48 * 1024 * 1024),
        cost_estimate=pl.CostEstimate(
            flops=2 * 8192 * start.shape[0] * 768, bytes_accessed=25_000_000, transcendentals=0
        ),
        name="scatter_rows",
    )(order, ids, start, *parts)


def product(left, right):
    return jnp.dot(left, right, preferred_element_type=F32)


def product_nt(left, right):
    return lax.dot_general(left, right, (((1,), (1,)), ((), ())), preferred_element_type=F32)


def product_tn(left, right):
    return lax.dot_general(left, right, (((0,), (0,)), ((), ())), preferred_element_type=F32)


def exact_mm(left, right):
    return jnp.dot(left, right, precision=exact_prec, preferred_element_type=F32)


def layer_norm(values_in, gain, shift):
    centre = jnp.mean(values_in, axis=-1, keepdims=True)
    cent = values_in - centre
    spread = jnp.mean(cent * cent, axis=-1, keepdims=True)
    return cent * lax.rsqrt(spread + 1e-05) * gain + shift


def layer_params(small_params, layer_idx):
    gain_rows = 2 * LAYERS + 1
    base_row = 2 * gain_rows + 8 * layer_idx
    model_width = small_params.shape[1]
    bias_qkv = jnp.concatenate(
        [small_params[base_row], jnp.zeros((model_width,), F32), small_params[base_row + 1]]
    )
    return (
        small_params[2 * layer_idx],
        small_params[2 * layer_idx + 1],
        small_params[gain_rows + 2 * layer_idx],
        small_params[gain_rows + 2 * layer_idx + 1],
        bias_qkv,
        small_params[base_row + 2],
        small_params[base_row + 3 : base_row + 7].reshape(-1),
        small_params[base_row + 7],
    )


def attend(queries_bf, key_values, doc_mask):
    model_width = queries_bf.shape[1]
    queries = queries_bf.reshape(-1, HEADS, HEAD_DIM)
    key_heads = key_values[:, :model_width].reshape(-1, HEADS, HEAD_DIM)
    scores = jnp.einsum("qhd,khd->hqk", queries, key_heads, preferred_element_type=F32) * 0.125
    scores = jnp.where(doc_mask[None], scores, -1e30)
    peak = jnp.max(scores, axis=-1, keepdims=True)
    expo = jnp.exp(scores - peak)
    return expo / jnp.sum(expo, axis=-1, keepdims=True)


def gather_pairs(own):
    core = swap(own, "c")
    far = z_flip(own)
    return jnp.concatenate([own, core, far, swap(far, "c")], axis=0)


def reduce_pairs(grad):
    span = grad.shape[0] // 4
    own, core, far, both = (grad[m * span : (m + 1) * span] for m in range(4))
    far = (far + swap(both, "c")).astype(BF)
    own = own + swap(core, "c")
    return own + wide(z_flip(far))


def layer_forward(residual, mats, params, doc_mask):
    w_qkv, w_proj, w_fc, w_out = mats
    gain_a, gain_b, shift_a, shift_b, bias_qkv, bias_proj, bias_fc, bias_out = params
    model_width = residual.shape[1]
    normed = layer_norm(residual, gain_a, shift_a).astype(BF)
    qkv_bf = (product(normed, w_qkv) + bias_qkv).astype(BF)
    key_values = gather_pairs(qkv_bf[:, model_width:])
    soft_probs = attend(qkv_bf[:, :model_width], key_values, doc_mask)
    value_heads = key_values[:, model_width:].reshape(-1, HEADS, HEAD_DIM)
    attended = jnp.einsum(
        "hqk,khd->qhd", soft_probs.astype(BF), value_heads, preferred_element_type=F32
    )
    attended = attended.reshape(-1, model_width).astype(BF)
    middle = residual + product(attended, w_proj) + bias_proj
    normed_b = layer_norm(middle, gain_b, shift_b).astype(BF)
    inner_pre = product(normed_b, w_fc) + bias_fc
    activated = jax.nn.gelu(inner_pre, approximate=True).astype(BF)
    result = middle + product(activated, w_out) + bias_out
    return (
        result,
        (residual, qkv_bf, key_values, attended, middle, normed_b, inner_pre, activated),
    )


def layer_backward(grad_in, kept_values, mats, params, doc_mask):
    residual, qkv_bf, key_values, attended, middle, normed_b, inner_pre, activated = kept_values
    w_qkv, w_proj, w_fc, w_out = mats
    gain_a, gain_b, shift_a, shift_b = params[:4]
    model_width = residual.shape[1]
    grad_out = grad_in.astype(BF)
    b_out = jnp.sum(wide(grad_out), axis=0)
    _, gelu_back = jax.vjp(lambda inner_in: jax.nn.gelu(inner_in, approximate=True), inner_pre)
    grad_inner = gelu_back(product_nt(grad_out, w_out))[0].astype(BF)
    b_fc = jnp.sum(wide(grad_inner), axis=0)
    _, norm_back_b = jax.vjp(layer_norm, middle, gain_b, shift_b)
    grad_mid, g_gain_b, g_shift_b = norm_back_b(product_nt(grad_inner, w_fc))
    grad_mid = grad_mid + grad_in
    grad_branch = grad_mid.astype(BF)
    b_proj = jnp.sum(wide(grad_branch), axis=0)
    grad_att = product_nt(grad_branch, w_proj).astype(BF)
    soft_probs = attend(qkv_bf[:, :model_width], key_values, doc_mask)
    seq_len = key_values.shape[0]
    queries = qkv_bf[:, :model_width].reshape(-1, HEADS, HEAD_DIM)
    key_heads = key_values[:, :model_width].reshape(seq_len, HEADS, HEAD_DIM)
    value_heads = key_values[:, model_width:].reshape(seq_len, HEADS, HEAD_DIM)
    grad_heads = grad_att.reshape(-1, HEADS, HEAD_DIM)
    grad_prob = jnp.einsum("qhd,khd->hqk", grad_heads, value_heads, preferred_element_type=F32)
    grad_score = soft_probs * (grad_prob - jnp.sum(soft_probs * grad_prob, axis=-1, keepdims=True))
    grad_score = grad_score.astype(BF)
    grad_query = (
        jnp.einsum("hqk,khd->qhd", grad_score, key_heads, preferred_element_type=F32).reshape(
            -1, model_width
        )
        * 0.125
    )
    grad_keys = (
        jnp.einsum("hqk,qhd->khd", grad_score, queries, preferred_element_type=F32).reshape(
            seq_len, model_width
        )
        * 0.125
    )
    grad_values = jnp.einsum(
        "hqk,qhd->khd", soft_probs.astype(BF), grad_heads, preferred_element_type=F32
    ).reshape(seq_len, model_width)
    grad_pairs = reduce_pairs(jnp.concatenate([grad_keys, grad_values], axis=1))
    grad_mixed = jnp.concatenate([grad_query, grad_pairs], axis=1).astype(BF)
    normed_a, norm_back_a = jax.vjp(layer_norm, residual, gain_a, shift_a)
    mixed_sums = jnp.sum(wide(grad_mixed), axis=0)
    grad_resid, g_gain_a, g_shift_a = norm_back_a(product_nt(grad_mixed, w_qkv))
    grad_resid = grad_resid + grad_mid
    bias_rows = jnp.concatenate(
        [
            jnp.stack([mixed_sums[:model_width], mixed_sums[2 * model_width :], b_proj]),
            b_fc.reshape(-1, model_width),
            b_out[None],
        ],
        axis=0,
    )
    return (
        grad_resid,
        (
            (normed_a.astype(BF), attended, normed_b, activated),
            (grad_mixed, grad_branch, grad_inner, grad_out),
        ),
        (g_gain_a, g_gain_b, g_shift_a, g_shift_b, bias_rows),
    )


def merge_stats(first_part, second_part):
    peak = jnp.maximum(first_part[0], second_part[0])
    summed = first_part[1] * jnp.exp(first_part[0] - peak) + second_part[1] * jnp.exp(
        second_part[0] - peak
    )
    return jnp.stack([peak, summed, first_part[2] + second_part[2]])


def adam_update(param, grad, first, second, rate, decay):
    first = first_decay * first + (1.0 - first_decay) * grad
    second = second_decay * second + (1.0 - second_decay) * grad * grad
    fixed_first = first / (1.0 - first_decay**STEP)
    fixed_second = second / (1.0 - second_decay**STEP)
    return (
        param - rate * (fixed_first / (jnp.sqrt(fixed_second) + adam_epsilon) + decay * param),
        first,
        second,
    )


def squared_blocks(flat):
    return flat.reshape(-1, BS, BS)


def gather_weights(packed, layer_idx, z_hi):
    from_there = permuted(packed, "zh", None, keep=lambda zh, c, y, zl, x: zh == layer_idx)
    mine = jnp.where(z_hi == layer_idx, packed, from_there)
    arrays = []
    for chunk in range(3):
        value = mine[chunk : chunk + 1]
        if chunk < 2:
            value = jnp.concatenate([value, swap(value, "zl")], axis=0)
            first, last = (("x", "y"), ("y", "x"))[chunk]
            value = jnp.concatenate(gather4(value, first), axis=0)
            arrays += gather4(value, last)
        else:
            value = jnp.concatenate(gather4(value, "x"), axis=0)
            value = jnp.concatenate(gather4(value, "y"), axis=0)
            arrays += [value, swap(value, "zl")]
    return arrays + [swap(value, "c") for value in arrays]


def reduce_weights(arrays, layer_idx, z_hi):
    blocks = []
    for chunk in range(3):
        mine, theirs = arrays[chunk], swap(arrays[3 + chunk], "c")
        axis, size, count = pieces_of(chunk)
        parts = [
            wide(mine[p * size : (p + 1) * size]) + wide(theirs[p * size : (p + 1) * size])
            for p in range(count)
        ]
        if chunk < 2:
            value = reduce4(parts, axis, BF)
            other = "x" if axis == "y" else "y"
            value = reduce4([value[2 * m : 2 * m + 2] for m in range(4)], other, BF)
            value = value[:1] + wide(swap(value[1:].astype(BF), "zl"))
        else:
            value = parts[0] + wide(swap(parts[1].astype(BF), "zl"))
            value = reduce4([value[4 * m : 4 * m + 4] for m in range(4)], "y", BF)
            value = reduce4([value[m : m + 1] for m in range(4)], "x", BF)
        blocks.append(value)
    value = jnp.concatenate(blocks, axis=0)
    from_there = permuted(value, "zh", None, keep=lambda zh, c, y, zl, x: zh != layer_idx)
    return value + from_there


def shards(
    token_ids,
    doc_ids,
    pick_slots,
    labels,
    vocab_table,
    vocab_first,
    vocab_second,
    positions,
    positions_first,
    positions_second,
    small_params,
    small_first,
    small_second,
    weights,
    stat_left,
    stat_right,
    root_left,
    root_right,
    anchor,
    fisher,
    owners,
):
    row_at = lax.axis_index("dp")
    seq_at = lax.axis_index("seq")
    z_hi, core = seq_at // 2, seq_at % 2
    y_at, zl_at, x_at = row_at // 8, (row_at // 4) % 2, row_at % 4
    span_len = token_ids.shape[1]
    model_width = small_params.shape[1]
    half_width = model_width // 2
    table_rows = vocab_table.shape[0]
    padded = -(-table_rows // 64) * 64
    vocab_start = row_at * 2 * table_rows
    shift_up, shift_down = jnp.array([0, 1, 2, 3]), jnp.array([0, 3, 2, 1])
    own_shift = jnp.where(core == 0, shift_up, shift_down)
    other_shift = jnp.where(core == 0, shift_down, shift_up)

    places = []
    for layer_idx in range(LAYERS):
        slots = []
        for kc in range(2):
            shift = own_shift if kc == 0 else other_shift
            for chunk in range(3):
                moves = jnp.array(inner_moves(chunk))
                at_y = (y_at + shift[moves[:, 0]]) % 4
                at_z = zl_at ^ moves[:, 1]
                at_x = (x_at + shift[moves[:, 2]]) % 4
                slots.append(((((core ^ kc) * 4 + at_y) * 2 + at_z) * 4 + at_x) * 3 + chunk)
        places.append(jnp.take(owners[layer_idx], jnp.concatenate(slots), axis=0))
    own_slots = (core * 32 + row_at) * 3 + jnp.arange(3)
    own_tiles = jnp.take(
        jnp.where(z_hi == 0, owners[0], owners[1]), own_slots, axis=0
    )
    own_odd = own_tiles % 2 == 1

    own_part = jnp.pad(vocab_table.astype(BF), ((0, padded - table_rows), (0, 0)))
    far_part = z_flip(own_part)
    both_parts = jnp.stack([own_part, far_part])
    near_parts = jnp.stack([swap(own_part, "c"), swap(far_part, "c")])
    table_bf = jnp.where(
        core == 0,
        jnp.concatenate([both_parts, near_parts], axis=2),
        jnp.concatenate([near_parts, both_parts], axis=2),
    ).reshape(2 * padded, model_width)
    vocab_rows = 2 * padded
    row_used = jnp.arange(vocab_rows) % padded < table_rows

    def local_row(ids):
        offset = ids - vocab_start
        inside = (offset >= 0) & (offset < 2 * table_rows)
        return jnp.where(inside, ((offset % 2) ^ z_hi) * padded + offset // 2, -1)

    packed = pack_blocks(squared_blocks(weights).astype(BF), own_odd)
    layer_weights = [
        assemble_layer(places[layer_idx], gather_weights(packed, layer_idx, z_hi))
        for layer_idx in range(LAYERS)
    ]
    all_params = [layer_params(small_params, layer_idx) for layer_idx in range(LAYERS)]

    far_y = (y_at + own_shift) % 4
    far_x = (x_at + own_shift) % 4
    far_z = zl_at ^ jnp.arange(2)
    rows_xyz = far_y[None, :, None] * 8 + far_z[None, None, :] * 4 + far_x[:, None, None]
    token_rows = local_row(jnp.take(token_ids, rows_xyz.reshape(-1), axis=0))
    spread_ids = jnp.broadcast_to(token_rows.reshape(-1, 1), (token_rows.size, LANES))
    found0, found1, found2, found3 = lookup(spread_ids, table_bf)

    def quarters(value):
        return jnp.split(value, 4, axis=0)

    def plain_reduce4(parts, axis):
        near = turn(parts[1] + turn(parts[2], axis, 1), axis, 1)
        return (parts[0] + near) + turn(parts[3], axis, -1)

    def last_pair(value):
        return value[:span_len] + swap(value[span_len:], "zl")

    looked = [
        last_pair(plain_reduce4(quarters(plain_reduce4(quarters(found0), "x")), "y")),
        last_pair(plain_reduce4(quarters(plain_reduce4(quarters(found1), "y")), "x")),
        plain_reduce4(quarters(plain_reduce4(quarters(found2 + swap(found3, "zl")), "x")), "y"),
    ]
    residual = wide(jnp.concatenate(looked, axis=1)) + positions

    doc_row = doc_ids[0]
    query_places = seq_at * span_len + jnp.arange(span_len)
    own_docs = lax.dynamic_slice_in_dim(doc_row, seq_at * span_len, span_len)
    part_order = seq_at ^ jnp.arange(4)
    key_places = (part_order[:, None] * span_len + jnp.arange(span_len)[None]).reshape(-1)
    key_docs = jnp.take(doc_row.reshape(4, span_len), part_order, axis=0).reshape(-1)
    doc_mask = (query_places[:, None] >= key_places[None, :]) & (
        own_docs[:, None] == key_docs[None, :]
    )
    kept_layers = []
    for layer_idx in range(LAYERS):
        residual, kept_values = layer_forward(
            residual, layer_weights[layer_idx], all_params[layer_idx], doc_mask
        )
        kept_layers.append(kept_values)
    gain_rows = 2 * LAYERS + 1
    final_norm, final_back = jax.vjp(
        layer_norm, residual, small_params[2 * LAYERS], small_params[gain_rows + 2 * LAYERS]
    )
    final_bf = final_norm.astype(BF)

    pick_dev = pick_slots.shape[1]
    half_picks = pick_dev // 2
    own_picks = lax.dynamic_index_in_dim(pick_slots, row_at, 0, keepdims=False)
    own_valid = own_picks >= 0
    pick_rows = jnp.maximum(own_picks, 0)
    chosen = jnp.where(own_valid[:, None], jnp.take(final_bf, pick_rows, axis=0), jnp.zeros((), BF))
    gathered = []
    for chunk in range(2):
        value = chosen[chunk * half_picks : (chunk + 1) * half_picks]
        value = jnp.concatenate([value, swap(value, "zl")], axis=0)
        first, last = (("x", "y"), ("y", "x"))[chunk]
        value = jnp.concatenate(gather4_direct(value, first), axis=0)
        gathered += gather4(value, last)
    gathered = jnp.concatenate(gathered, axis=0)
    rows_yxz = jnp.transpose(rows_xyz, (1, 0, 2)).reshape(-1)
    rows_xyz = rows_xyz.reshape(-1)

    def in_order(table):
        return jnp.concatenate(
            [
                jnp.take(table[:, :half_picks], rows_yxz, axis=0).reshape(-1),
                jnp.take(table[:, half_picks:], rows_xyz, axis=0).reshape(-1),
            ]
        )

    valid_all = in_order(pick_slots) >= 0
    label_rows = local_row(in_order(labels))
    logits = jnp.where(row_used[None, :], product_nt(gathered, table_bf), -1e30)
    hits = label_rows[:, None] == jnp.arange(vocab_rows)[None, :]
    peak = jnp.max(logits, axis=1)
    exp_total = jnp.sum(jnp.exp(logits - peak[:, None]), axis=1)
    target = jnp.sum(jnp.where(hits, logits, 0.0), axis=1)
    stats = jnp.stack([peak, exp_total, target])
    devices = jnp.arange(32)
    at_y = jnp.take(own_shift, (devices // 8 - y_at) % 4)
    at_x = jnp.take(own_shift, (devices % 4 - x_at) % 4)
    at_z = (devices // 4) % 2 ^ zl_at
    back_y = (at_y * 4 + at_x) * 2 + at_z
    back_x = (at_x * 4 + at_y) * 2 + at_z

    def reorder(value, first_order, second_order):
        value = value.reshape(value.shape[0], 2, 32, half_picks)
        return jnp.stack(
            [jnp.take(value[:, 0], first_order, axis=1), jnp.take(value[:, 1], second_order, axis=1)],
            axis=1,
        ).reshape(value.shape[0], -1)

    stats = reorder(stats, back_y, back_x)
    stats = merge_stats(stats, swap(stats, "zl"))
    for axis in ("x", "y"):
        one, two, three = (crossed(stats, axis, mask) for mask in (1, 2, 3))
        stats = merge_stats(merge_stats(stats, one), merge_stats(two, three))
    stats = reorder(stats, rows_yxz, rows_xyz)
    log_total = stats[0] + jnp.log(stats[1])
    losses = jnp.where(valid_all, log_total - stats[2], 0.0).reshape(2, 32, half_picks)
    loss_own = jnp.sum(losses[:, 0])
    count_own = jnp.sum(own_valid.astype(F32))
    grad_logits = jnp.where(
        valid_all[:, None], jnp.exp(logits - log_total[:, None]) - hits.astype(F32), 0.0
    ).astype(BF)
    head_grad = product_tn(grad_logits, gathered)
    grad_gathered = product(grad_logits, table_bf)
    grad_chosen = []
    for chunk in range(2):
        value = grad_gathered[chunk * 32 * half_picks : (chunk + 1) * 32 * half_picks]
        first, last = (("y", "x"), ("x", "y"))[chunk]
        value = reduce4(quarters(value), first, BF)
        value = reduce4_direct(quarters(value), last, F32)
        grad_chosen.append(value[:half_picks] + swap(value[half_picks:], "zl"))
    grad_chosen = jnp.concatenate(grad_chosen, axis=0)
    grad_final = (
        jnp.zeros((span_len, model_width), F32)
        .at[pick_rows]
        .add(jnp.where(own_valid[:, None], grad_chosen, 0.0))
    )
    grad_resid, g_final_gain, g_final_shift = final_back(grad_final)

    own_parts = [None] * LAYERS
    small_parts = [None] * LAYERS
    for layer_idx in reversed(range(LAYERS)):
        grad_resid, (lefts, rights), small_part = layer_backward(
            grad_resid,
            kept_layers[layer_idx],
            layer_weights[layer_idx],
            all_params[layer_idx],
            doc_mask,
        )
        own_parts[layer_idx] = reduce_weights(
            weight_grads(places[layer_idx], lefts, rights), layer_idx, z_hi
        )
        small_parts[layer_idx] = small_part
    own_blocks = unpack_blocks(jnp.where(z_hi == 0, own_parts[0], own_parts[1]), own_odd)

    grad_bf = grad_resid.astype(BF)
    columns = [grad_bf[:, at : at + 256] for at in range(0, model_width, 256)]

    def joined(parts):
        return jnp.concatenate(parts, axis=0)

    pair0 = joined([columns[0], swap(columns[0], "zl")])
    spread0 = joined(gather4(joined(gather4(pair0, "y")), "x"))
    pair1 = joined([columns[1], swap(columns[1], "zl")])
    spread1 = joined(gather4(joined(gather4(pair1, "x")), "y"))
    spread2 = joined(gather4(joined(gather4(columns[2], "y")), "x"))
    spread3 = swap(spread2, "zl")
    steps = jnp.arange(16)
    step_y = jnp.take(own_shift, (steps // 4 - y_at) % 4)
    step_x = jnp.take(own_shift, (steps % 4 - x_at) % 4)
    order = jnp.stack([step_x * 4 + step_y, step_y * 4 + step_x]).astype(jnp.int32)
    grad_table, pos_sum = scatter_rows(
        order, token_rows.reshape(16, 1, 512), head_grad, (spread0, spread1, spread2, spread3)
    )
    left_half, right_half = grad_table[:, :half_width], grad_table[:, half_width:]
    grad_half = jnp.where(core == 0, left_half, right_half) + swap(
        jnp.where(core == 0, right_half, left_half), "c"
    )
    far_grad = z_flip(grad_half[padded : padded + table_rows].astype(BF))
    grad_own = grad_half[:table_rows] + wide(far_grad)

    gain_list = []
    shift_list = []
    for layer_idx in range(LAYERS):
        gain_list += [small_parts[layer_idx][0], small_parts[layer_idx][1]]
        shift_list += [small_parts[layer_idx][2], small_parts[layer_idx][3]]
    scalars = jnp.zeros((model_width,), F32).at[0].set(loss_own).at[1].set(count_own)
    small_grad = jnp.concatenate(
        [jnp.stack(gain_list + [g_final_gain]), jnp.stack(shift_list + [g_final_shift])]
        + [small_parts[layer_idx][4] for layer_idx in range(LAYERS)]
        + [scalars[None]],
        axis=0,
    )
    small_all = sum_everywhere(small_grad)
    small_sum, ce_sum, pick_count = small_all[:-1], small_all[-1, 0], small_all[-1, 1]

    g_table = grad_own / pick_count
    g_pos = pos_sum / pick_count
    g_small = small_sum / pick_count
    g_ce = own_blocks.reshape(weights.shape) / pick_count
    g_blocks = g_ce + ewc_weight * fisher * (weights - anchor)
    first_row = row_at == 0
    first_seq = seq_at == 0
    local_squares = jnp.sum(g_table * g_table) + jnp.sum(g_blocks * g_blocks)
    local_squares = local_squares + jnp.where(first_row, jnp.sum(g_pos * g_pos), 0.0)
    local_squares = local_squares + jnp.where(
        first_row & first_seq, jnp.sum(g_small * g_small), 0.0
    )
    grad_norm = jnp.sqrt(sum_everywhere(jnp.broadcast_to(local_squares, (8, LANES)))[0, 0])
    factor = jnp.minimum(1.0, clip_bound / grad_norm)
    table_new, table_first, table_second = adam_update(
        vocab_table, factor * g_table, vocab_first, vocab_second, table_rate, decay_rate
    )
    pos_new, pos_first, pos_second = adam_update(
        positions, factor * g_pos, positions_first, positions_second, table_rate, 0.0
    )
    small_new, small_first_new, small_second_new = adam_update(
        small_params, factor * g_small, small_first, small_second, small_rate, 0.0
    )
    block_grad = factor * g_blocks

    def products(grad, root_l, root_r):
        return exact_mm(grad, grad.T), exact_mm(grad.T, grad), exact_mm(exact_mm(root_l, grad), root_r)

    left_mm, right_mm, direction = jax.vmap(products)(
        squared_blocks(g_blocks), squared_blocks(root_left), squared_blocks(root_right)
    )
    direction = (factor * direction).reshape(weights.shape)
    mean_square = jnp.mean(direction * direction, axis=1, keepdims=True)
    direction = direction * lax.rsqrt(mean_square + graft_epsilon)
    weights_new = weights - shampoo_rate * (direction + decay_rate * weights)
    square = factor * factor
    left_new = stat_decay * stat_left + (1.0 - stat_decay) * (
        square * left_mm.reshape(weights.shape)
    )
    right_new = stat_decay * stat_right + (1.0 - stat_decay) * (
        square * right_mm.reshape(weights.shape)
    )
    fisher_new = fisher_decay * fisher + (1.0 - fisher_decay) * g_ce * g_ce
    return (
        ce_sum,
        pick_count,
        grad_norm,
        table_new,
        table_first,
        table_second,
        pos_new,
        pos_first,
        pos_second,
        small_new,
        small_first_new,
        small_second_new,
        weights_new,
        left_new,
        right_new,
        block_grad,
        fisher_new,
    )


def solution(mesh):
    split = P(("seq", "dp"), None)
    table = P("dp", "seq")
    in_specs = (
        (P(None, "seq"), P("dp", None), P(None, "seq"), P(None, "seq"))
        + (table,) * 3
        + (P("seq", None),) * 3
        + (P(),) * 3
        + (split,) * 7
        + (P(),)
    )
    out_specs = (
        (P(),) * 3 + (table,) * 3 + (P("seq", None),) * 3 + (P(),) * 3 + (split,) * 5
    )
    return jax.shard_map(shards, mesh=mesh, in_specs=in_specs, out_specs=out_specs, check_vma=False)
```

```python
import functools

import jax
import jax.numpy as jnp
from jax import lax
from jax.experimental import pallas as pl
from jax.experimental.pallas import tpu as pltpu
from jax.sharding import PartitionSpec as P

HEADS = 12
HEAD_DIM = 64
LAYERS = 2
BS = 192
STEP = 10
PACK = 288
LANES = 128
HALF = 96
SLOTS = 64

exact_prec = lax.Precision.HIGHEST
clip_bound = 0.02
ewc_weight = 1000000.0
fisher_decay = 0.8
first_decay = 0.9
second_decay = 0.999
adam_epsilon = 1e-08
table_rate = 0.05
small_rate = 0.1
decay_rate = 0.1
stat_decay = 0.9
shampoo_rate = 0.02
graft_epsilon = 1e-06

BF = jnp.bfloat16
F32 = jnp.float32


def line(zh, c, y, zl, x):
    return (zh * 2 + c) * 32 + y * 8 + zl * 4 + x


def moved(axis, step, zh, c, y, zl, x):
    z = zh * 2 + zl
    if axis == "x":
        x = step(x, c)
    elif axis == "y":
        y = step(y, c)
    elif axis == "z":
        z = step(z, c)
        zh, zl = z // 2, z % 2
    elif axis == "c":
        c = 1 - c
    elif axis == "zl":
        zl = 1 - zl
    elif axis == "zh":
        zh = 1 - zh
    return zh, c, y, zl, x


COORDS = [
    (zh, c, y, zl, x)
    for zh in range(2)
    for c in range(2)
    for y in range(4)
    for zl in range(2)
    for x in range(4)
]


def permuted(value, axis, step, keep=None):
    pairs = [
        (line(*at), line(*moved(axis, step, *at))) for at in COORDS if keep is None or keep(*at)
    ]
    return lax.ppermute(value, ("seq", "dp"), pairs)


def turn(value, axis, amount):
    return permuted(value, axis, lambda at, c: (at + (amount if c == 0 else -amount)) % 4)


def swap(value, axis):
    return permuted(value, axis, None)


def z_flip(value):
    return turn(turn(value, "z", 1), "z", 1)


def gather4(value, axis):
    near = turn(value, axis, -1)
    other = turn(value, axis, 1)
    return [value, near, turn(near, axis, -1), other]


def wide(value):
    return value.astype(F32)


def reduce4(parts, axis, kind):
    first = turn(parts[2].astype(kind), axis, 1)
    onward = (wide(parts[1]) + wide(first)).astype(kind)
    near = turn(onward, axis, 1)
    other = turn(parts[3].astype(kind), axis, -1)
    return wide(parts[0]) + wide(near) + wide(other)


def sum_everywhere(value):
    shape, share = value.shape, value.size // len(COORDS)
    parts = exchanged(value.reshape(len(COORDS), share), ("seq", "dp"))
    total = jnp.sum(parts, axis=0, keepdims=True)
    spread = jnp.broadcast_to(total, (len(COORDS), share))
    return exchanged(spread, ("seq", "dp")).reshape(shape)


def exchanged(value, axes):
    return lax.all_to_all(value, axes, 0, 0, tiled=True)


def pack_blocks(blocks, odd):
    odd = odd[:, None, None]
    main = jnp.where(odd, blocks[:, :, BS - LANES :], blocks[:, :, :LANES])
    half = jnp.where(odd, blocks[:, :, : BS - LANES], blocks[:, :, LANES:])
    top, low = half[:, :HALF], half[:, HALF:]
    rest = jnp.concatenate([jnp.where(odd, low, top), jnp.where(odd, top, low)], axis=2)
    return jnp.concatenate([main, rest], axis=1)


def unpack_blocks(packed):
    main, rest = packed[:, :BS], packed[:, BS:]
    half = jnp.concatenate([rest[:, :, : LANES // 2], rest[:, :, LANES // 2 :]], axis=1)
    return jnp.concatenate([main, half], axis=2)


def pieces_of(chunk):
    return (("y", 8, 4), ("x", 8, 4), ("zl", 16, 2))[chunk]


def inner_moves(chunk):
    if chunk == 0:
        return [(my, kz, mx) for my in range(4) for mx in range(4) for kz in range(2)]
    if chunk == 1:
        return [(my, kz, mx) for mx in range(4) for my in range(4) for kz in range(2)]
    return [(my, kz, mx) for kz in range(2) for my in range(4) for mx in range(4)]


MATRICES = ((0, 4, 12), (48, 4, 4), (64, 4, 16), (128, 16, 4))


def assemble_kernel(places, *refs):
    arrays, outs, (halves, sems) = refs[:20], refs[20:24], refs[24:]
    at = 0
    for array in arrays:

        def fetch(q, carry, array=array, at=at):
            tile = places[at + q]
            pltpu.make_async_copy(array.at[q, pl.ds(BS, HALF)], halves.at[tile], sems.at[4]).start()
            for which, out in enumerate(outs):
                base, tall, across = MATRICES[which]

                @pl.when((tile >= base) & (tile < base + tall * across))
                def _(out=out, base=base, across=across, which=which):
                    row, col = (tile - base) // across, (tile - base) % across
                    left = pl.multiple_of((col // 2) * 2 * BS + (col % 2) * 2 * LANES, LANES)
                    target = out.at[pl.ds(pl.multiple_of(row * BS, HALF), BS), pl.ds(left, LANES)]
                    pltpu.make_async_copy(array.at[q, pl.ds(0, BS)], target, sems.at[which]).start()

            return carry

        lax.fori_loop(0, array.shape[0], fetch, 0)
        at += array.shape[0]
    pltpu.make_async_copy(halves, halves, sems.at[4]).wait()
    for which, out in enumerate(outs):
        most = out.at[:, pl.ds(0, 2 * out.shape[1] // 3)]
        pltpu.make_async_copy(most, most, sems.at[which]).wait()
    left_lanes = lax.broadcasted_iota(jnp.int32, (HALF, LANES), 1) < LANES // 2
    for out, (base, tall, across) in zip(outs, MATRICES, strict=True):
        pairs = across // 2

        def place(t, carry, out=out, base=base, pairs=pairs):
            row = pl.multiple_of((t // pairs) * BS, HALF)
            col = pl.multiple_of((t % pairs) * 2 * BS + LANES, LANES)
            he, ho = wide(halves[base + 2 * t]), wide(halves[base + 2 * t + 1])
            out[pl.ds(row, HALF), pl.ds(col, LANES)] = jnp.where(left_lanes, he, ho).astype(BF)
            out[pl.ds(row + HALF, HALF), pl.ds(col, LANES)] = pltpu.roll(
                jnp.where(left_lanes, ho, he), LANES // 2, 1
            ).astype(BF)
            return carry

        lax.fori_loop(0, tall * pairs, place, 0, unroll=2)


def assemble_layer(places, arrays):
    shapes = [jax.ShapeDtypeStruct((t * BS, a * BS), BF) for _, t, a in MATRICES]
    return pl.pallas_call(
        assemble_kernel,
        grid_spec=pltpu.PrefetchScalarGridSpec(
            num_scalar_prefetch=1,
            grid=(),
            in_specs=[pl.BlockSpec(memory_space=pl.ANY)] * len(arrays),
            out_specs=[pl.BlockSpec(memory_space=pltpu.VMEM)] * 4,
            scratch_shapes=[pltpu.VMEM((BS, HALF, LANES), BF), pltpu.SemaphoreType.DMA((5,))],
        ),
        out_shape=shapes,
        compiler_params=pltpu.CompilerParams(vmem_limit_bytes=40 * 1024 * 1024),
        cost_estimate=pl.CostEstimate(flops=0, bytes_accessed=29_000_000, transcendentals=0),
        name="assemble",
    )(places, *arrays)


LEFT_ROWS = (768, 768, 768, 3072)
RIGHT_ROWS = (2304, 768, 3072, 768)


def tile_rows(tiles):
    matrix = sum((tiles >= base).astype(jnp.int32) for base, _, _ in MATRICES[1:])
    offset = tiles - jnp.take(jnp.array([m[0] for m in MATRICES]), matrix)
    across = jnp.take(jnp.array([m[2] for m in MATRICES]), matrix)
    left_base = jnp.take(jnp.array([0, 768, 1536, 2304]), matrix)
    right_base = jnp.take(jnp.array([0, 2304, 3072, 6144]), matrix)
    return jnp.stack(
        [left_base + BS * (offset // across), right_base + BS * (offset % across)]
    ).astype(jnp.int32)


def weight_grad_kernel(rows, *refs):
    sources, outs, (lefts, rights, sems) = refs[:16], refs[16:19], refs[19:]
    for part in range(2):
        for stack, sizes, first in ((lefts, LEFT_ROWS, 0), (rights, RIGHT_ROWS, 4)):
            at = 0
            for index, size in enumerate(sizes):
                pltpu.make_async_copy(
                    sources[8 * part + first + index],
                    stack.at[pl.ds(at, size), pl.ds(256 * part, 256)],
                    sems.at[first // 4],
                ).start()
                at += size
    rights[pl.ds(sum(RIGHT_ROWS), 64)] = jnp.zeros((64, 512), BF)
    pltpu.make_async_copy(lefts, lefts, sems.at[0]).wait()
    filled = rights.at[pl.ds(0, sum(RIGHT_ROWS))]
    pltpu.make_async_copy(filled, filled, sems.at[1]).wait()
    left_lanes = lax.broadcasted_iota(jnp.int32, (HALF, LANES), 1) < LANES // 2
    for chunk, out in enumerate(outs):

        def tile(q, carry, chunk=chunk, out=out):
            left = lefts[pl.ds(pl.multiple_of(rows[0, 32 * chunk + q], 64), BS)]
            right = rights[pl.ds(pl.multiple_of(rows[1, 32 * chunk + q], 64), 256)]
            value = lax.dot_general(
                left, right, (((1,), (1,)), ((), ())), preferred_element_type=F32
            )
            out[q, :BS] = value[:, :LANES].astype(BF)
            rest = value[:, LANES:]
            low = pltpu.roll(rest[HALF:], LANES // 2, 1)
            out[q, BS:] = jnp.where(left_lanes, rest[:HALF], low).astype(BF)
            return carry

        lax.fori_loop(0, 32, tile, 0, unroll=2)


def weight_grads(tiles, lefts, rights):
    own = [value.T for value in (*lefts, *rights)]
    other = [swap(value, "c") for value in own]
    return pl.pallas_call(
        weight_grad_kernel,
        grid_spec=pltpu.PrefetchScalarGridSpec(
            num_scalar_prefetch=1,
            grid=(),
            in_specs=[pl.BlockSpec(memory_space=pl.ANY)] * 16,
            out_specs=[pl.BlockSpec(memory_space=pltpu.VMEM)] * 3,
            scratch_shapes=[
                pltpu.VMEM((sum(LEFT_ROWS), 512), BF),
                pltpu.VMEM((sum(RIGHT_ROWS) + 64, 512), BF),
                pltpu.SemaphoreType.DMA((2,)),
            ],
        ),
        out_shape=[jax.ShapeDtypeStruct((32, PACK, LANES), BF)] * 3,
        compiler_params=pltpu.CompilerParams(vmem_limit_bytes=40 * 1024 * 1024),
        cost_estimate=pl.CostEstimate(
            flops=2 * 512 * 96 * BS * BS, bytes_accessed=20_000_000, transcendentals=0
        ),
        name="weight_grads",
    )(tile_rows(tiles), *own, *other)


def lookup_kernel(ids, table, out0, out1, out2, out3):
    rows = table.shape[0]
    lane = lax.broadcasted_iota(jnp.int32, (ids.shape[0], LANES), 1)
    held = ids[...]
    hot = jnp.concatenate(
        [jnp.where(held == lane + at, 1.0, 0.0).astype(BF) for at in range(0, rows, LANES)], axis=1
    )
    found = jnp.dot(hot, table[...], preferred_element_type=F32).astype(BF)
    out0[...] = found[:, :256]
    out1[...] = found[:, 256:512]
    out2[...] = found[:256, 512:]
    out3[...] = found[256:, 512:]


def lookup(ids, table):
    tokens = ids.shape[0]
    steps = tokens // 512
    return pl.pallas_call(
        lookup_kernel,
        grid=(steps,),
        in_specs=[
            pl.BlockSpec((512, LANES), lambda t: (t, 0)),
            pl.BlockSpec(table.shape, lambda t: (0, 0)),
        ],
        out_specs=[
            pl.BlockSpec((512, 256), lambda t: (t, 0)),
            pl.BlockSpec((512, 256), lambda t: ((t % 4) * 4 + t // 4, 0)),
            pl.BlockSpec((256, 256), lambda t: (t, 0)),
            pl.BlockSpec((256, 256), lambda t: (t, 0)),
        ],
        out_shape=[
            jax.ShapeDtypeStruct((tokens, 256), BF),
            jax.ShapeDtypeStruct((tokens, 256), BF),
            jax.ShapeDtypeStruct((tokens // 2, 256), BF),
            jax.ShapeDtypeStruct((tokens // 2, 256), BF),
        ],
        compiler_params=pltpu.CompilerParams(vmem_limit_bytes=40 * 1024 * 1024),
        cost_estimate=pl.CostEstimate(
            flops=2 * tokens * table.shape[0] * 768, bytes_accessed=20_000_000, transcendentals=0
        ),
        name="lookup",
    )(ids, table)


def scatter_kernel(ids, start, part0, part1, part2, part3, out):
    @pl.when(pl.program_id(0) == 0)
    def _():
        out[...] = start[...]

    rows, tokens = out.shape[0], ids.shape[2]
    place = lax.broadcasted_iota(jnp.int32, (rows, tokens), 0)
    hot = jnp.where(place == ids[0], 1.0, 0.0).astype(BF)
    last = jnp.concatenate([part2[...], part3[...]], axis=0)
    for at, part in enumerate((part0[...], part1[...], last)):
        cols = slice(at * 256, (at + 1) * 256)
        out[:, cols] += jnp.dot(hot, part, preferred_element_type=F32)


def scatter_rows(ids, start, parts):
    return pl.pallas_call(
        scatter_kernel,
        grid=(16,),
        in_specs=[
            pl.BlockSpec((1, 1, 512), lambda t: (t, 0, 0)),
            pl.BlockSpec(start.shape, lambda t: (0, 0)),
            pl.BlockSpec((512, 256), lambda t: (t, 0)),
            pl.BlockSpec((512, 256), lambda t: ((t % 4) * 4 + t // 4, 0)),
            pl.BlockSpec((256, 256), lambda t: (t, 0)),
            pl.BlockSpec((256, 256), lambda t: (t, 0)),
        ],
        out_specs=pl.BlockSpec(start.shape, lambda t: (0, 0)),
        out_shape=jax.ShapeDtypeStruct(start.shape, F32),
        compiler_params=pltpu.CompilerParams(vmem_limit_bytes=48 * 1024 * 1024),
        cost_estimate=pl.CostEstimate(
            flops=2 * 8192 * start.shape[0] * 768, bytes_accessed=25_000_000, transcendentals=0
        ),
        name="scatter_rows",
    )(ids, start, *parts)


def pick_rows_kernel(ids, table, out):
    rows = table.shape[0]
    lane = lax.broadcasted_iota(jnp.int32, (ids.shape[0], LANES), 1)
    held = ids[...]
    hot = jnp.concatenate(
        [jnp.where(held == lane + at, 1.0, 0.0).astype(BF) for at in range(0, rows, LANES)], axis=1
    )
    out[...] = jnp.dot(hot, table[...], preferred_element_type=F32).astype(BF)


def pick_table_rows(ids, table):
    count, width = ids.size, table.shape[1]
    spread = jnp.broadcast_to(ids.reshape(-1, 1), (count, LANES))
    tall = min(512, count)
    return pl.pallas_call(
        pick_rows_kernel,
        grid=(count // tall,),
        in_specs=[
            pl.BlockSpec((tall, LANES), lambda t: (t, 0)),
            pl.BlockSpec(table.shape, lambda t: (0, 0)),
        ],
        out_specs=pl.BlockSpec((tall, width), lambda t: (t, 0)),
        out_shape=jax.ShapeDtypeStruct((count, width), BF),
        compiler_params=pltpu.CompilerParams(vmem_limit_bytes=40 * 1024 * 1024),
        cost_estimate=pl.CostEstimate(
            flops=2 * count * table.shape[0] * width, bytes_accessed=8_000_000, transcendentals=0
        ),
        name="pick_table_rows",
    )(spread, table)


def add_rows_kernel(ids, start, rows, out):
    @pl.when(pl.program_id(0) == 0)
    def _():
        out[...] = start[...]

    place = lax.broadcasted_iota(jnp.int32, (out.shape[0], ids.shape[2]), 0)
    hot = jnp.where(place == ids[0], 1.0, 0.0).astype(BF)
    out[...] += jnp.dot(hot, rows[...], preferred_element_type=F32)


def add_table_rows(ids, start, rows):
    count, width = rows.shape
    return pl.pallas_call(
        add_rows_kernel,
        grid=(count // 512,),
        in_specs=[
            pl.BlockSpec((1, 1, 512), lambda t: (t, 0, 0)),
            pl.BlockSpec(start.shape, lambda t: (0, 0)),
            pl.BlockSpec((512, width), lambda t: (t, 0)),
        ],
        out_specs=pl.BlockSpec(start.shape, lambda t: (0, 0)),
        out_shape=jax.ShapeDtypeStruct(start.shape, F32),
        compiler_params=pltpu.CompilerParams(vmem_limit_bytes=48 * 1024 * 1024),
        cost_estimate=pl.CostEstimate(
            flops=2 * count * start.shape[0] * width, bytes_accessed=14_000_000, transcendentals=0
        ),
        name="add_table_rows",
    )(ids.reshape(-1, 1, 512), start, rows)


def product(left, right):
    return jnp.dot(left, right, preferred_element_type=F32)


def product_nt(left, right):
    return lax.dot_general(left, right, (((1,), (1,)), ((), ())), preferred_element_type=F32)


def product_tn(left, right):
    return lax.dot_general(left, right, (((0,), (0,)), ((), ())), preferred_element_type=F32)


def exact_mm(left, right):
    return jnp.dot(left, right, precision=exact_prec, preferred_element_type=F32)


def layer_norm(values_in, gain, shift):
    centre = jnp.mean(values_in, axis=-1, keepdims=True)
    cent = values_in - centre
    spread = jnp.mean(cent * cent, axis=-1, keepdims=True)
    return cent * lax.rsqrt(spread + 1e-05) * gain + shift


def layer_params(small_params, layer_idx):
    gain_rows = 2 * LAYERS + 1
    base_row = 2 * gain_rows + 8 * layer_idx
    model_width = small_params.shape[1]
    bias_qkv = jnp.concatenate(
        [small_params[base_row], jnp.zeros((model_width,), F32), small_params[base_row + 1]]
    )
    return (
        small_params[2 * layer_idx],
        small_params[2 * layer_idx + 1],
        small_params[gain_rows + 2 * layer_idx],
        small_params[gain_rows + 2 * layer_idx + 1],
        bias_qkv,
        small_params[base_row + 2],
        small_params[base_row + 3 : base_row + 7].reshape(-1),
        small_params[base_row + 7],
    )


def attend(queries_bf, key_values, doc_mask):
    model_width = queries_bf.shape[1]
    queries = queries_bf.reshape(-1, HEADS, HEAD_DIM)
    key_heads = key_values[:, :model_width].reshape(-1, HEADS, HEAD_DIM)
    scores = jnp.einsum("qhd,khd->hqk", queries, key_heads, preferred_element_type=F32) * 0.125
    scores = jnp.where(doc_mask[None], scores, -1e30)
    peak = jnp.max(scores, axis=-1, keepdims=True)
    expo = jnp.exp(scores - peak)
    return expo / jnp.sum(expo, axis=-1, keepdims=True)


def gather_pairs(own):
    core = swap(own, "c")
    far = z_flip(own)
    return jnp.concatenate([own, core, far, swap(far, "c")], axis=0)


def reduce_pairs(grad):
    span = grad.shape[0] // 4
    own, core, far, both = (grad[m * span : (m + 1) * span] for m in range(4))
    far = (far + swap(both, "c")).astype(BF)
    own = own + swap(core, "c")
    return own + wide(z_flip(far))


def layer_forward(residual, mats, params, doc_mask):
    w_qkv, w_proj, w_fc, w_out = mats
    gain_a, gain_b, shift_a, shift_b, bias_qkv, bias_proj, bias_fc, bias_out = params
    model_width = residual.shape[1]
    normed = layer_norm(residual, gain_a, shift_a).astype(BF)
    qkv_bf = (product(normed, w_qkv) + bias_qkv).astype(BF)
    key_values = gather_pairs(qkv_bf[:, model_width:])
    soft_probs = attend(qkv_bf[:, :model_width], key_values, doc_mask)
    value_heads = key_values[:, model_width:].reshape(-1, HEADS, HEAD_DIM)
    attended = jnp.einsum(
        "hqk,khd->qhd", soft_probs.astype(BF), value_heads, preferred_element_type=F32
    )
    attended = attended.reshape(-1, model_width).astype(BF)
    middle = residual + product(attended, w_proj) + bias_proj
    normed_b = layer_norm(middle, gain_b, shift_b).astype(BF)
    inner_pre = product(normed_b, w_fc) + bias_fc
    activated = jax.nn.gelu(inner_pre, approximate=True).astype(BF)
    result = middle + product(activated, w_out) + bias_out
    return (
        result,
        (residual, qkv_bf, key_values, attended, middle, normed_b, inner_pre, activated),
    )


def layer_backward(grad_in, kept_values, mats, params, doc_mask):
    residual, qkv_bf, key_values, attended, middle, normed_b, inner_pre, activated = kept_values
    w_qkv, w_proj, w_fc, w_out = mats
    gain_a, gain_b, shift_a, shift_b = params[:4]
    model_width = residual.shape[1]
    grad_out = grad_in.astype(BF)
    b_out = jnp.sum(wide(grad_out), axis=0)
    _, gelu_back = jax.vjp(lambda inner_in: jax.nn.gelu(inner_in, approximate=True), inner_pre)
    grad_inner = gelu_back(product_nt(grad_out, w_out))[0].astype(BF)
    b_fc = jnp.sum(wide(grad_inner), axis=0)
    _, norm_back_b = jax.vjp(layer_norm, middle, gain_b, shift_b)
    grad_mid, g_gain_b, g_shift_b = norm_back_b(product_nt(grad_inner, w_fc))
    grad_mid = grad_mid + grad_in
    grad_branch = grad_mid.astype(BF)
    b_proj = jnp.sum(wide(grad_branch), axis=0)
    grad_att = product_nt(grad_branch, w_proj).astype(BF)
    soft_probs = attend(qkv_bf[:, :model_width], key_values, doc_mask)
    seq_len = key_values.shape[0]
    queries = qkv_bf[:, :model_width].reshape(-1, HEADS, HEAD_DIM)
    key_heads = key_values[:, :model_width].reshape(seq_len, HEADS, HEAD_DIM)
    value_heads = key_values[:, model_width:].reshape(seq_len, HEADS, HEAD_DIM)
    grad_heads = grad_att.reshape(-1, HEADS, HEAD_DIM)
    grad_prob = jnp.einsum("qhd,khd->hqk", grad_heads, value_heads, preferred_element_type=F32)
    grad_score = soft_probs * (grad_prob - jnp.sum(soft_probs * grad_prob, axis=-1, keepdims=True))
    grad_score = grad_score.astype(BF)
    grad_query = (
        jnp.einsum("hqk,khd->qhd", grad_score, key_heads, preferred_element_type=F32).reshape(
            -1, model_width
        )
        * 0.125
    )
    grad_keys = (
        jnp.einsum("hqk,qhd->khd", grad_score, queries, preferred_element_type=F32).reshape(
            seq_len, model_width
        )
        * 0.125
    )
    grad_values = jnp.einsum(
        "hqk,qhd->khd", soft_probs.astype(BF), grad_heads, preferred_element_type=F32
    ).reshape(seq_len, model_width)
    grad_pairs = reduce_pairs(jnp.concatenate([grad_keys, grad_values], axis=1))
    grad_mixed = jnp.concatenate([grad_query, grad_pairs], axis=1).astype(BF)
    normed_a, norm_back_a = jax.vjp(layer_norm, residual, gain_a, shift_a)
    mixed_sums = jnp.sum(wide(grad_mixed), axis=0)
    grad_resid, g_gain_a, g_shift_a = norm_back_a(product_nt(grad_mixed, w_qkv))
    grad_resid = grad_resid + grad_mid
    bias_rows = jnp.concatenate(
        [
            jnp.stack([mixed_sums[:model_width], mixed_sums[2 * model_width :], b_proj]),
            b_fc.reshape(-1, model_width),
            b_out[None],
        ],
        axis=0,
    )
    return (
        grad_resid,
        (
            (normed_a.astype(BF), attended, normed_b, activated),
            (grad_mixed, grad_branch, grad_inner, grad_out),
        ),
        (g_gain_a, g_gain_b, g_shift_a, g_shift_b, bias_rows),
    )


def adam_update(param, grad, first, second, rate, decay):
    first = first_decay * first + (1.0 - first_decay) * grad
    second = second_decay * second + (1.0 - second_decay) * grad * grad
    fixed_first = first / (1.0 - first_decay**STEP)
    fixed_second = second / (1.0 - second_decay**STEP)
    return (
        param - rate * (fixed_first / (jnp.sqrt(fixed_second) + adam_epsilon) + decay * param),
        first,
        second,
    )


def squared_blocks(flat):
    return flat.reshape(-1, BS, BS)


def gather_weights(packed, layer_idx, z_hi):
    from_there = permuted(packed, "zh", None, keep=lambda zh, c, y, zl, x: zh == layer_idx)
    mine = jnp.where(z_hi == layer_idx, packed, from_there)
    arrays = []
    for chunk in range(3):
        value = mine[chunk : chunk + 1]
        if chunk < 2:
            value = jnp.concatenate([value, swap(value, "zl")], axis=0)
            first, last = (("x", "y"), ("y", "x"))[chunk]
            value = jnp.concatenate(gather4(value, first), axis=0)
            arrays += gather4(value, last)
        else:
            value = jnp.concatenate(gather4(value, "x"), axis=0)
            value = jnp.concatenate(gather4(value, "y"), axis=0)
            arrays += [value, swap(value, "zl")]
    return arrays + [swap(value, "c") for value in arrays]


def reduce_weights(arrays, layer_idx, z_hi):
    blocks = []
    for chunk in range(3):
        axis, size, count = pieces_of(chunk)
        parts = [arrays[chunk][p * size : (p + 1) * size] for p in range(count)]
        if chunk < 2:
            value = reduce4(parts, axis, BF)
            other = "x" if axis == "y" else "y"
            value = reduce4([value[2 * m : 2 * m + 2] for m in range(4)], other, BF)
            value = value[:1] + wide(swap(value[1:].astype(BF), "zl"))
        else:
            value = wide(parts[0]) + wide(swap(parts[1], "zl"))
            value = reduce4([value[4 * m : 4 * m + 4] for m in range(4)], "y", BF)
            value = reduce4([value[m : m + 1] for m in range(4)], "x", BF)
        blocks.append(value)
    value = jnp.concatenate(blocks, axis=0)
    from_there = permuted(value, "zh", None, keep=lambda zh, c, y, zl, x: zh != layer_idx)
    return value + from_there


def shards(
    token_ids,
    doc_ids,
    pick_slots,
    labels,
    vocab_table,
    vocab_first,
    vocab_second,
    positions,
    positions_first,
    positions_second,
    small_params,
    small_first,
    small_second,
    weights,
    stat_left,
    stat_right,
    root_left,
    root_right,
    anchor,
    fisher,
    owners,
):
    row_at = lax.axis_index("dp")
    seq_at = lax.axis_index("seq")
    z_hi, core = seq_at // 2, seq_at % 2
    y_at, zl_at, x_at = row_at // 8, (row_at // 4) % 2, row_at % 4
    span_len = token_ids.shape[1]
    model_width = small_params.shape[1]
    half_width = model_width // 2
    table_rows = vocab_table.shape[0]
    padded = -(-table_rows // 64) * 64
    vocab_start = row_at * 2 * table_rows
    shift_up, shift_down = jnp.array([0, 1, 2, 3]), jnp.array([0, 3, 2, 1])
    own_shift = jnp.where(core == 0, shift_up, shift_down)
    other_shift = jnp.where(core == 0, shift_down, shift_up)

    places = []
    for layer_idx in range(LAYERS):
        slots = []
        for kc in range(2):
            shift = own_shift if kc == 0 else other_shift
            for chunk in range(3):
                moves = jnp.array(inner_moves(chunk))
                at_y = (y_at + shift[moves[:, 0]]) % 4
                at_z = zl_at ^ moves[:, 1]
                at_x = (x_at + shift[moves[:, 2]]) % 4
                slots.append(((((core ^ kc) * 4 + at_y) * 2 + at_z) * 4 + at_x) * 3 + chunk)
        places.append(jnp.take(owners[layer_idx], jnp.concatenate(slots), axis=0))
    own_slots = (core * 32 + row_at) * 3 + jnp.arange(3)
    own_tiles = jnp.take(
        jnp.where(z_hi == 0, owners[0], owners[1]), own_slots, axis=0
    )
    own_odd = own_tiles % 2 == 1

    own_part = jnp.pad(vocab_table.astype(BF), ((0, padded - table_rows), (0, 0)))
    far_part = z_flip(own_part)
    both_parts = jnp.stack([own_part, far_part])
    near_parts = jnp.stack([swap(own_part, "c"), swap(far_part, "c")])
    table_bf = jnp.where(
        core == 0,
        jnp.concatenate([both_parts, near_parts], axis=2),
        jnp.concatenate([near_parts, both_parts], axis=2),
    ).reshape(2 * padded, model_width)
    vocab_rows = 2 * padded
    row_used = jnp.arange(vocab_rows) % padded < table_rows

    def local_row(ids):
        offset = ids - vocab_start
        inside = (offset >= 0) & (offset < 2 * table_rows)
        return jnp.where(inside, ((offset % 2) ^ z_hi) * padded + offset // 2, -1)

    packed = pack_blocks(squared_blocks(weights).astype(BF), own_odd)
    layer_weights = []
    for layer_idx in range(LAYERS):
        arrays = gather_weights(packed, layer_idx, z_hi)
        packed, arrays[2], arrays[6], arrays[9] = lax.optimization_barrier(
            (packed, arrays[2], arrays[6], arrays[9])
        )
        layer_weights.append(assemble_layer(places[layer_idx], arrays))
    all_params = [layer_params(small_params, layer_idx) for layer_idx in range(LAYERS)]

    sequences = token_ids.shape[0]
    shard_of = token_ids // (2 * table_rows)
    held_by = (shard_of[:, None, :] == jnp.arange(sequences)[None, :, None]).astype(BF)
    before = (jnp.arange(span_len)[:, None] <= jnp.arange(span_len)[None, :]).astype(BF)
    ranks = product(held_by.reshape(-1, span_len), before).reshape(held_by.shape).astype(jnp.int32) - 1
    crowded = jnp.max(ranks[:, :, -1]) >= SLOTS
    crowded = jnp.broadcast_to(crowded.astype(F32), (8, LANES))
    crowded = jnp.maximum(crowded, swap(crowded, "c"))
    crowded = jnp.maximum(crowded, swap(crowded, "zh"))[0, 0] > 0.0
    all_rows = local_row(token_ids)
    own_ranks = lax.dynamic_index_in_dim(ranks, row_at, 1, keepdims=False)
    slots = jnp.arange(SLOTS)
    in_slot = (own_ranks[:, None, :] == slots[None, :, None]) & (all_rows >= 0)[:, None, :]
    slot_rows = jnp.sum(jnp.where(in_slot, all_rows[:, None, :] + 1, 0), axis=2) - 1
    arrived = exchanged(pick_table_rows(slot_rows, table_bf), "dp")
    my_shards = lax.dynamic_index_in_dim(shard_of, row_at, 0, keepdims=False)
    my_ranks = lax.dynamic_index_in_dim(ranks, row_at, 0, keepdims=False)
    my_rank = jnp.sum(jnp.where(my_shards[None, :] == jnp.arange(sequences)[:, None], my_ranks, 0), axis=0)
    my_slots = jnp.where(my_rank < SLOTS, my_shards * SLOTS + my_rank, -1)
    slot_hot = my_slots[:, None] == jnp.arange(sequences * SLOTS)[None, :]
    looked = product(slot_hot.astype(BF), arrived)

    far_y = (y_at + own_shift) % 4
    far_x = (x_at + own_shift) % 4
    far_z = zl_at ^ jnp.arange(2)
    rows_xyz = far_y[None, :, None] * 8 + far_z[None, None, :] * 4 + far_x[:, None, None]
    crowd_rows = jnp.where(own_ranks >= SLOTS, all_rows, -1)
    crowd_rows = jnp.take(crowd_rows, rows_xyz.reshape(-1), axis=0)

    def quarters(value):
        return jnp.split(value, 4, axis=0)

    def dense_rows():
        spread_ids = jnp.broadcast_to(crowd_rows.reshape(-1, 1), (crowd_rows.size, LANES))
        found0, found1, found2, found3 = lookup(spread_ids, table_bf)

        def plain_reduce4(parts, axis):
            near = turn(parts[1] + turn(parts[2], axis, 1), axis, 1)
            return (parts[0] + near) + turn(parts[3], axis, -1)

        def last_pair(value):
            return value[:span_len] + swap(value[span_len:], "zl")

        parts = [
            last_pair(plain_reduce4(quarters(plain_reduce4(quarters(found0), "x")), "y")),
            last_pair(plain_reduce4(quarters(plain_reduce4(quarters(found1), "y")), "x")),
            plain_reduce4(quarters(plain_reduce4(quarters(found2 + swap(found3, "zl")), "x")), "y"),
        ]
        return wide(jnp.concatenate(parts, axis=1))

    looked = looked + lax.cond(crowded, dense_rows, lambda: jnp.zeros((span_len, model_width), F32))
    residual = looked + positions

    doc_row = doc_ids[0]
    query_places = seq_at * span_len + jnp.arange(span_len)
    own_docs = lax.dynamic_slice_in_dim(doc_row, seq_at * span_len, span_len)
    part_order = seq_at ^ jnp.arange(4)
    key_places = (part_order[:, None] * span_len + jnp.arange(span_len)[None]).reshape(-1)
    key_docs = jnp.take(doc_row.reshape(4, span_len), part_order, axis=0).reshape(-1)
    doc_mask = (query_places[:, None] >= key_places[None, :]) & (
        own_docs[:, None] == key_docs[None, :]
    )
    kept_layers = []
    for layer_idx in range(LAYERS):
        residual, kept_values = layer_forward(
            residual, layer_weights[layer_idx], all_params[layer_idx], doc_mask
        )
        kept_layers.append(kept_values)
    gain_rows = 2 * LAYERS + 1
    final_norm, final_back = jax.vjp(
        layer_norm, residual, small_params[2 * LAYERS], small_params[gain_rows + 2 * LAYERS]
    )
    final_bf = final_norm.astype(BF)

    pick_dev = pick_slots.shape[1]
    own_picks = lax.dynamic_index_in_dim(pick_slots, row_at, 0, keepdims=False)
    own_valid = own_picks >= 0
    pick_rows = jnp.maximum(own_picks, 0)
    chosen = jnp.where(own_valid[:, None], jnp.take(final_bf, pick_rows, axis=0), jnp.zeros((), BF))
    gathered = exchanged(jnp.tile(chosen, (sequences, 1)), "dp")
    valid_all = pick_slots.reshape(-1) >= 0
    label_rows = local_row(labels.reshape(-1))
    logits = jnp.where(row_used[None, :], product_nt(gathered, table_bf), -1e30)
    hits = label_rows[:, None] == jnp.arange(vocab_rows)[None, :]
    peak = jnp.max(logits, axis=1)
    exp_total = jnp.sum(jnp.exp(logits - peak[:, None]), axis=1)
    target = jnp.sum(jnp.where(hits, logits, 0.0), axis=1)
    stats = jnp.stack([peak, exp_total, target]).reshape(1, -1)
    stats = exchanged(jnp.tile(stats, (sequences, 1)), "dp").reshape(sequences, 3, -1)
    top = jnp.max(stats[:, 0], axis=0)
    log_total = top + jnp.log(jnp.sum(stats[:, 1] * jnp.exp(stats[:, 0] - top[None]), axis=0))
    losses = jnp.where(valid_all, log_total - jnp.sum(stats[:, 2], axis=0), 0.0)
    loss_own = jnp.sum(lax.dynamic_slice_in_dim(losses, row_at * pick_dev, pick_dev))
    count_own = jnp.sum(own_valid.astype(F32))
    grad_logits = jnp.where(
        valid_all[:, None], jnp.exp(logits - log_total[:, None]) - hits.astype(F32), 0.0
    ).astype(BF)
    head_grad = product_tn(grad_logits, gathered)
    grad_chosen = exchanged(product(grad_logits, table_bf).astype(BF), "dp")
    grad_chosen = jnp.sum(wide(grad_chosen.reshape(sequences, pick_dev, model_width)), axis=0)
    grad_final = (
        jnp.zeros((span_len, model_width), F32)
        .at[pick_rows]
        .add(jnp.where(own_valid[:, None], grad_chosen, 0.0))
    )
    grad_resid, g_final_gain, g_final_shift = final_back(grad_final)

    own_parts = [None] * LAYERS
    small_parts = [None] * LAYERS
    for layer_idx in reversed(range(LAYERS)):
        grad_resid, (lefts, rights), small_part = layer_backward(
            grad_resid,
            kept_layers[layer_idx],
            layer_weights[layer_idx],
            all_params[layer_idx],
            doc_mask,
        )
        tiles = weight_grads(places[layer_idx][:96], lefts, rights)
        if layer_idx:
            grad_resid, tiles = lax.optimization_barrier((grad_resid, tiles))
        own_parts[layer_idx] = reduce_weights(tiles, layer_idx, z_hi)
        small_parts[layer_idx] = small_part
    own_blocks = unpack_blocks(jnp.where(z_hi == 0, own_parts[0], own_parts[1]))

    grad_bf = grad_resid.astype(BF)
    slot_grads = product_tn(slot_hot.astype(BF), grad_bf).astype(BF)
    grad_table = add_table_rows(slot_rows, head_grad, exchanged(slot_grads, "dp"))

    def dense_grads():
        columns = [grad_bf[:, at : at + 256] for at in range(0, model_width, 256)]

        def joined(parts):
            return jnp.concatenate(parts, axis=0)

        pair0 = joined([columns[0], swap(columns[0], "zl")])
        spread0 = joined(gather4(joined(gather4(pair0, "y")), "x"))
        pair1 = joined([columns[1], swap(columns[1], "zl")])
        spread1 = joined(gather4(joined(gather4(pair1, "x")), "y"))
        spread2 = joined(gather4(joined(gather4(columns[2], "y")), "x"))
        spread3 = swap(spread2, "zl")
        return scatter_rows(
            crowd_rows.reshape(16, 1, 512), grad_table, (spread0, spread1, spread2, spread3)
        )

    grad_table = lax.cond(crowded, dense_grads, lambda: grad_table)
    pos_parts = exchanged(grad_resid, "dp").reshape(sequences, -1, model_width)
    pos_own = jnp.sum(pos_parts, axis=0)
    pos_sum = exchanged(jnp.tile(pos_own, (sequences, 1)), "dp")
    left_half, right_half = grad_table[:, :half_width], grad_table[:, half_width:]
    grad_half = jnp.where(core == 0, left_half, right_half) + swap(
        jnp.where(core == 0, right_half, left_half), "c"
    )
    far_grad = z_flip(grad_half[padded : padded + table_rows].astype(BF))
    grad_own = grad_half[:table_rows] + wide(far_grad)

    gain_list = []
    shift_list = []
    for layer_idx in range(LAYERS):
        gain_list += [small_parts[layer_idx][0], small_parts[layer_idx][1]]
        shift_list += [small_parts[layer_idx][2], small_parts[layer_idx][3]]
    scalars = jnp.zeros((model_width,), F32).at[0].set(loss_own).at[1].set(count_own)
    small_grad = jnp.concatenate(
        [jnp.stack(gain_list + [g_final_gain]), jnp.stack(shift_list + [g_final_shift])]
        + [small_parts[layer_idx][4] for layer_idx in range(LAYERS)]
        + [scalars[None], jnp.zeros((5, model_width), F32)],
        axis=0,
    )
    small_all = sum_everywhere(small_grad)
    rows = small_params.shape[0]
    small_sum, ce_sum, pick_count = small_all[:rows], small_all[rows, 0], small_all[rows, 1]

    g_table = grad_own / pick_count
    g_pos = pos_sum / pick_count
    g_small = small_sum / pick_count
    g_ce = own_blocks.reshape(weights.shape) / pick_count
    g_blocks = g_ce + ewc_weight * fisher * (weights - anchor)
    g_pos_own = pos_own / pick_count
    local_squares = jnp.sum(g_table * g_table) + jnp.sum(g_blocks * g_blocks)
    local_squares = local_squares + jnp.sum(g_pos_own * g_pos_own)
    local_squares = local_squares + jnp.where(
        (row_at == 0) & (seq_at == 0), jnp.sum(g_small * g_small), 0.0
    )
    all_squares = exchanged(jnp.broadcast_to(local_squares, (len(COORDS), LANES)), ("seq", "dp"))
    grad_norm = jnp.sqrt(jnp.sum(all_squares[:, 0]))
    factor = jnp.minimum(1.0, clip_bound / grad_norm)
    table_new, table_first, table_second = adam_update(
        vocab_table, factor * g_table, vocab_first, vocab_second, table_rate, decay_rate
    )
    pos_new, pos_first, pos_second = adam_update(
        positions, factor * g_pos, positions_first, positions_second, table_rate, 0.0
    )
    small_new, small_first_new, small_second_new = adam_update(
        small_params, factor * g_small, small_first, small_second, small_rate, 0.0
    )
    block_grad = factor * g_blocks

    def products(grad, root_l, root_r):
        return exact_mm(grad, grad.T), exact_mm(grad.T, grad), exact_mm(exact_mm(root_l, grad), root_r)

    left_mm, right_mm, direction = jax.vmap(products)(
        squared_blocks(g_blocks), squared_blocks(root_left), squared_blocks(root_right)
    )
    direction = (factor * direction).reshape(weights.shape)
    mean_square = jnp.mean(direction * direction, axis=1, keepdims=True)
    direction = direction * lax.rsqrt(mean_square + graft_epsilon)
    weights_new = weights - shampoo_rate * (direction + decay_rate * weights)
    square = factor * factor
    left_new = stat_decay * stat_left + (1.0 - stat_decay) * (
        square * left_mm.reshape(weights.shape)
    )
    right_new = stat_decay * stat_right + (1.0 - stat_decay) * (
        square * right_mm.reshape(weights.shape)
    )
    fisher_new = fisher_decay * fisher + (1.0 - fisher_decay) * g_ce * g_ce
    return (
        ce_sum,
        pick_count,
        grad_norm,
        table_new,
        table_first,
        table_second,
        pos_new,
        pos_first,
        pos_second,
        small_new,
        small_first_new,
        small_second_new,
        weights_new,
        left_new,
        right_new,
        block_grad,
        fisher_new,
    )


def solution(mesh):
    split = P(("seq", "dp"), None)
    table = P("dp", "seq")
    in_specs = (
        (P(None, "seq"), P("dp", None), P(None, "seq"), P(None, "seq"))
        + (table,) * 3
        + (P("seq", None),) * 3
        + (P(),) * 3
        + (split,) * 7
        + (P(),)
    )
    out_specs = (
        (P(),) * 3 + (table,) * 3 + (P("seq", None),) * 3 + (P(),) * 3 + (split,) * 5
    )
    return jax.shard_map(shards, mesh=mesh, in_specs=in_specs, out_specs=out_specs, check_vma=False)
```

```python
import functools

import jax
import jax.numpy as jnp
from jax import lax
from jax.experimental import pallas as pl
from jax.experimental.pallas import tpu as pltpu
from jax.sharding import PartitionSpec as P

HEADS = 12
HEAD_DIM = 64
LAYERS = 2
BS = 192
STEP = 10
LANES = 128
HALF = 96
SLOTS = 64

exact_prec = lax.Precision.HIGHEST
clip_bound = 0.02
ewc_weight = 1000000.0
fisher_decay = 0.8
first_decay = 0.9
second_decay = 0.999
adam_epsilon = 1e-08
table_rate = 0.05
small_rate = 0.1
decay_rate = 0.1
stat_decay = 0.9
shampoo_rate = 0.02
graft_epsilon = 1e-06

BF = jnp.bfloat16
F32 = jnp.float32


def line(zh, c, y, zl, x):
    return (zh * 2 + c) * 32 + y * 8 + zl * 4 + x


def moved(axis, step, zh, c, y, zl, x):
    z = zh * 2 + zl
    if axis == "x":
        x = step(x, c)
    elif axis == "y":
        y = step(y, c)
    elif axis == "z":
        z = step(z, c)
        zh, zl = z // 2, z % 2
    elif axis == "c":
        c = 1 - c
    elif axis == "zl":
        zl = 1 - zl
    elif axis == "zh":
        zh = 1 - zh
    return zh, c, y, zl, x


COORDS = [
    (zh, c, y, zl, x)
    for zh in range(2)
    for c in range(2)
    for y in range(4)
    for zl in range(2)
    for x in range(4)
]


def permuted(value, axis, step, keep=None):
    pairs = [
        (line(*at), line(*moved(axis, step, *at))) for at in COORDS if keep is None or keep(*at)
    ]
    return lax.ppermute(value, ("seq", "dp"), pairs)


def turn(value, axis, amount):
    return permuted(value, axis, lambda at, c: (at + (amount if c == 0 else -amount)) % 4)


def swap(value, axis):
    return permuted(value, axis, None)


def z_flip(value):
    return turn(turn(value, "z", 1), "z", 1)


def gather4(value, axis):
    near = turn(value, axis, -1)
    other = turn(value, axis, 1)
    return [value, near, turn(near, axis, -1), other]


def wide(value):
    return value.astype(F32)


def exchanged(value, axes):
    return lax.all_to_all(value, axes, 0, 0, tiled=True)


def joined(*parts):
    return jnp.concatenate(parts, axis=0)


MATRICES = ((0, 4, 12), (48, 4, 4), (64, 4, 16), (128, 16, 4))
SHAPES = [(tall * BS, across * BS) for _, tall, across in MATRICES]


def tile_places(tiles):
    matrix = sum((tiles >= base).astype(jnp.int32) for base, _, _ in MATRICES[1:])
    offset = tiles - jnp.take(jnp.array([m[0] for m in MATRICES]), matrix)
    across = jnp.take(jnp.array([m[2] for m in MATRICES]), matrix)
    odd = tiles % 2
    column = BS * (offset % across) - odd * (LANES // 2)
    return jnp.stack([matrix, BS * (offset // across), column, odd]).astype(jnp.int32)


def spread_kernel(places, tiles, *outs):
    for out in outs:

        def clear(at, carry, out=out):
            out[pl.ds(pl.multiple_of(at * HALF, HALF), HALF)] = jnp.zeros((HALF, out.shape[1]), BF)
            return carry

        lax.fori_loop(0, out.shape[0] // HALF, clear, 0)
    for k in range(3):
        for which, out in enumerate(outs):

            @pl.when(places[0, k] == which)
            def _(out=out, k=k):
                row = pl.ds(pl.multiple_of(places[1, k], 64), BS)
                col = pl.ds(pl.multiple_of(places[2, k], LANES), 2 * LANES)
                value = tiles[k]
                value = jnp.where(places[3, k] == 1, pltpu.roll(value, LANES // 2, 1), value)
                out[row, col] = (wide(out[row, col]) + value).astype(BF)


def spread_tiles(places, tiles):
    return pl.pallas_call(
        spread_kernel,
        grid_spec=pltpu.PrefetchScalarGridSpec(
            num_scalar_prefetch=1,
            grid=(),
            in_specs=[pl.BlockSpec(memory_space=pltpu.VMEM)],
            out_specs=[pl.BlockSpec(memory_space=pltpu.VMEM)] * 4,
        ),
        out_shape=[jax.ShapeDtypeStruct(shape, BF) for shape in SHAPES],
        compiler_params=pltpu.CompilerParams(vmem_limit_bytes=32 * 1024 * 1024),
        cost_estimate=pl.CostEstimate(flops=0, bytes_accessed=15_000_000, transcendentals=0),
        name="spread_tiles",
    )(places, tiles)


def cut_kernel(places, *refs):
    matrices, out, (held, sem) = refs[:8], refs[8], refs[9:]
    for k in range(3):
        for which, matrix in enumerate(matrices):

            @pl.when(places[0, k] == which)
            def _(matrix=matrix, k=k):
                row = pl.ds(pl.multiple_of(places[1, k], 64), BS)
                col = pl.ds(pl.multiple_of(places[2, k], LANES), 2 * LANES)
                pltpu.make_async_copy(matrix.at[row, col], held.at[k], sem).start()

    pltpu.make_async_copy(held, held, sem).wait()
    for k in range(3):
        value = held[k]
        value = jnp.where(places[3, k] == 1, pltpu.roll(value, 2 * LANES - LANES // 2, 1), value)
        out[k] = value[:, :BS]


def cut_tiles(places, matrices):
    return pl.pallas_call(
        cut_kernel,
        grid_spec=pltpu.PrefetchScalarGridSpec(
            num_scalar_prefetch=1,
            grid=(),
            in_specs=[pl.BlockSpec(memory_space=pl.ANY)] * 8,
            out_specs=pl.BlockSpec(memory_space=pltpu.VMEM),
            scratch_shapes=[pltpu.VMEM((3, BS, 2 * LANES), F32), pltpu.SemaphoreType.DMA],
        ),
        out_shape=jax.ShapeDtypeStruct((3, BS, BS), F32),
        compiler_params=pltpu.CompilerParams(vmem_limit_bytes=16 * 1024 * 1024),
        cost_estimate=pl.CostEstimate(flops=0, bytes_accessed=1_000_000, transcendentals=0),
        name="cut_tiles",
    )(places, *matrices)


def lookup_kernel(ids, table, out0, out1, out2, out3):
    rows = table.shape[0]
    lane = lax.broadcasted_iota(jnp.int32, (ids.shape[0], LANES), 1)
    held = ids[...]
    hot = jnp.concatenate(
        [jnp.where(held == lane + at, 1.0, 0.0).astype(BF) for at in range(0, rows, LANES)], axis=1
    )
    found = jnp.dot(hot, table[...], preferred_element_type=F32).astype(BF)
    out0[...] = found[:, :256]
    out1[...] = found[:, 256:512]
    out2[...] = found[:256, 512:]
    out3[...] = found[256:, 512:]


def lookup(ids, table):
    tokens = ids.shape[0]
    steps = tokens // 512
    return pl.pallas_call(
        lookup_kernel,
        grid=(steps,),
        in_specs=[
            pl.BlockSpec((512, LANES), lambda t: (t, 0)),
            pl.BlockSpec(table.shape, lambda t: (0, 0)),
        ],
        out_specs=[
            pl.BlockSpec((512, 256), lambda t: (t, 0)),
            pl.BlockSpec((512, 256), lambda t: ((t % 4) * 4 + t // 4, 0)),
            pl.BlockSpec((256, 256), lambda t: (t, 0)),
            pl.BlockSpec((256, 256), lambda t: (t, 0)),
        ],
        out_shape=[
            jax.ShapeDtypeStruct((tokens, 256), BF),
            jax.ShapeDtypeStruct((tokens, 256), BF),
            jax.ShapeDtypeStruct((tokens // 2, 256), BF),
            jax.ShapeDtypeStruct((tokens // 2, 256), BF),
        ],
        compiler_params=pltpu.CompilerParams(vmem_limit_bytes=40 * 1024 * 1024),
        cost_estimate=pl.CostEstimate(
            flops=2 * tokens * table.shape[0] * 768, bytes_accessed=20_000_000, transcendentals=0
        ),
        name="lookup",
    )(ids, table)


def scatter_kernel(ids, start, part0, part1, part2, part3, out):
    @pl.when(pl.program_id(0) == 0)
    def _():
        out[...] = start[...]

    rows, tokens = out.shape[0], ids.shape[2]
    place = lax.broadcasted_iota(jnp.int32, (rows, tokens), 0)
    hot = jnp.where(place == ids[0], 1.0, 0.0).astype(BF)
    last = jnp.concatenate([part2[...], part3[...]], axis=0)
    for at, part in enumerate((part0[...], part1[...], last)):
        cols = slice(at * 256, (at + 1) * 256)
        out[:, cols] += jnp.dot(hot, part, preferred_element_type=F32)


def scatter_rows(ids, start, parts):
    return pl.pallas_call(
        scatter_kernel,
        grid=(16,),
        in_specs=[
            pl.BlockSpec((1, 1, 512), lambda t: (t, 0, 0)),
            pl.BlockSpec(start.shape, lambda t: (0, 0)),
            pl.BlockSpec((512, 256), lambda t: (t, 0)),
            pl.BlockSpec((512, 256), lambda t: ((t % 4) * 4 + t // 4, 0)),
            pl.BlockSpec((256, 256), lambda t: (t, 0)),
            pl.BlockSpec((256, 256), lambda t: (t, 0)),
        ],
        out_specs=pl.BlockSpec(start.shape, lambda t: (0, 0)),
        out_shape=jax.ShapeDtypeStruct(start.shape, F32),
        compiler_params=pltpu.CompilerParams(vmem_limit_bytes=48 * 1024 * 1024),
        cost_estimate=pl.CostEstimate(
            flops=2 * 8192 * start.shape[0] * 768, bytes_accessed=25_000_000, transcendentals=0
        ),
        name="scatter_rows",
    )(ids, start, *parts)


def pick_rows_kernel(ids, table, out):
    rows = table.shape[0]
    lane = lax.broadcasted_iota(jnp.int32, (ids.shape[0], LANES), 1)
    held = ids[...]
    hot = jnp.concatenate(
        [jnp.where(held == lane + at, 1.0, 0.0).astype(BF) for at in range(0, rows, LANES)], axis=1
    )
    out[...] = jnp.dot(hot, table[...], preferred_element_type=F32).astype(BF)


def pick_table_rows(ids, table):
    count, width = ids.size, table.shape[1]
    spread = jnp.broadcast_to(ids.reshape(-1, 1), (count, LANES))
    tall = min(512, count)
    return pl.pallas_call(
        pick_rows_kernel,
        grid=(count // tall,),
        in_specs=[
            pl.BlockSpec((tall, LANES), lambda t: (t, 0)),
            pl.BlockSpec(table.shape, lambda t: (0, 0)),
        ],
        out_specs=pl.BlockSpec((tall, width), lambda t: (t, 0)),
        out_shape=jax.ShapeDtypeStruct((count, width), BF),
        compiler_params=pltpu.CompilerParams(vmem_limit_bytes=40 * 1024 * 1024),
        cost_estimate=pl.CostEstimate(
            flops=2 * count * table.shape[0] * width, bytes_accessed=8_000_000, transcendentals=0
        ),
        name="pick_table_rows",
    )(spread, table)


def add_rows_kernel(ids, start, rows, out):
    @pl.when(pl.program_id(0) == 0)
    def _():
        out[...] = start[...]

    place = lax.broadcasted_iota(jnp.int32, (out.shape[0], ids.shape[2]), 0)
    hot = jnp.where(place == ids[0], 1.0, 0.0).astype(BF)
    out[...] += jnp.dot(hot, rows[...], preferred_element_type=F32)


def add_table_rows(ids, start, rows):
    count, width = rows.shape
    return pl.pallas_call(
        add_rows_kernel,
        grid=(count // 512,),
        in_specs=[
            pl.BlockSpec((1, 1, 512), lambda t: (t, 0, 0)),
            pl.BlockSpec(start.shape, lambda t: (0, 0)),
            pl.BlockSpec((512, width), lambda t: (t, 0)),
        ],
        out_specs=pl.BlockSpec(start.shape, lambda t: (0, 0)),
        out_shape=jax.ShapeDtypeStruct(start.shape, F32),
        compiler_params=pltpu.CompilerParams(vmem_limit_bytes=48 * 1024 * 1024),
        cost_estimate=pl.CostEstimate(
            flops=2 * count * start.shape[0] * width, bytes_accessed=14_000_000, transcendentals=0
        ),
        name="add_table_rows",
    )(ids.reshape(-1, 1, 512), start, rows)


def product(left, right):
    return jnp.dot(left, right, preferred_element_type=F32)


def product_nt(left, right):
    return lax.dot_general(left, right, (((1,), (1,)), ((), ())), preferred_element_type=F32)


def product_tn(left, right):
    return lax.dot_general(left, right, (((0,), (0,)), ((), ())), preferred_element_type=F32)


def exact_mm(left, right):
    return jnp.dot(left, right, precision=exact_prec, preferred_element_type=F32)


def layer_norm(values_in, gain, shift):
    centre = jnp.mean(values_in, axis=-1, keepdims=True)
    cent = values_in - centre
    spread = jnp.mean(cent * cent, axis=-1, keepdims=True)
    return cent * lax.rsqrt(spread + 1e-05) * gain + shift


def layer_params(small_params, layer_idx):
    gain_rows = 2 * LAYERS + 1
    base_row = 2 * gain_rows + 8 * layer_idx
    model_width = small_params.shape[1]
    bias_qkv = jnp.concatenate(
        [small_params[base_row], jnp.zeros((model_width,), F32), small_params[base_row + 1]]
    )
    return (
        small_params[2 * layer_idx],
        small_params[2 * layer_idx + 1],
        small_params[gain_rows + 2 * layer_idx],
        small_params[gain_rows + 2 * layer_idx + 1],
        bias_qkv,
        small_params[base_row + 2],
        small_params[base_row + 3 : base_row + 7].reshape(-1),
        small_params[base_row + 7],
    )


def attend(queries_bf, key_values, doc_mask):
    model_width = queries_bf.shape[1]
    queries = queries_bf.reshape(-1, HEADS, HEAD_DIM)
    key_heads = key_values[:, :model_width].reshape(-1, HEADS, HEAD_DIM)
    scores = jnp.einsum("qhd,khd->hqk", queries, key_heads, preferred_element_type=F32) * 0.125
    scores = jnp.where(doc_mask[None], scores, -1e30)
    peak = jnp.max(scores, axis=-1, keepdims=True)
    expo = jnp.exp(scores - peak)
    return expo / jnp.sum(expo, axis=-1, keepdims=True)


def layer_forward(residual, mats, params, doc_mask):
    w_qkv, w_proj, w_fc, w_out = mats
    gain_a, gain_b, shift_a, shift_b, bias_qkv, bias_proj, bias_fc, bias_out = params
    model_width = residual.shape[1]
    normed = layer_norm(residual, gain_a, shift_a).astype(BF)
    qkv_bf = (product(normed, w_qkv) + bias_qkv).astype(BF)
    own_pairs = qkv_bf[:, model_width:]
    core_pairs = swap(own_pairs, "c")
    far_pairs = z_flip(own_pairs)
    both_pairs = swap(far_pairs, "c")
    key_values = jnp.concatenate([own_pairs, core_pairs, far_pairs, both_pairs], axis=0)
    soft_probs = attend(qkv_bf[:, :model_width], key_values, doc_mask)
    value_heads = key_values[:, model_width:].reshape(-1, HEADS, HEAD_DIM)
    attended = jnp.einsum(
        "hqk,khd->qhd", soft_probs.astype(BF), value_heads, preferred_element_type=F32
    )
    attended = attended.reshape(-1, model_width).astype(BF)
    middle = residual + product(attended, w_proj) + bias_proj
    normed_b = layer_norm(middle, gain_b, shift_b).astype(BF)
    inner_pre = product(normed_b, w_fc) + bias_fc
    activated = jax.nn.gelu(inner_pre, approximate=True).astype(BF)
    result = middle + product(activated, w_out) + bias_out
    return (
        result,
        (residual, normed, qkv_bf, key_values, attended, middle, normed_b, inner_pre, activated),
    )


def layer_backward(grad_in, kept_values, mats, params, doc_mask, earlier):
    residual, normed, qkv_bf, key_values, attended, middle, normed_b, inner_pre, activated = (
        kept_values
    )
    w_qkv, w_proj, w_fc, w_out = mats
    gain_a, gain_b, shift_a, shift_b = params[:4]
    model_width = residual.shape[1]
    grad_out = grad_in.astype(BF)
    b_out = jnp.sum(wide(grad_out), axis=0)
    _, gelu_back = jax.vjp(lambda inner_in: jax.nn.gelu(inner_in, approximate=True), inner_pre)
    grad_inner = gelu_back(product_nt(grad_out, w_out))[0].astype(BF)
    b_fc = jnp.sum(wide(grad_inner), axis=0)
    early = product_tn(normed_b, grad_inner), product_tn(activated, grad_out)
    grad_inner, early = lax.optimization_barrier((grad_inner, early))
    if earlier is not None:
        early, first_earlier = lax.optimization_barrier((early, earlier[0]))
    early = lax.psum(early, ("seq", "dp"))
    _, norm_back_b = jax.vjp(layer_norm, middle, gain_b, shift_b)
    grad_mid, g_gain_b, g_shift_b = norm_back_b(product_nt(grad_inner, w_fc))
    grad_mid = grad_mid + grad_in
    grad_branch = grad_mid.astype(BF)
    b_proj = jnp.sum(wide(grad_branch), axis=0)
    grad_att = product_nt(grad_branch, w_proj).astype(BF)
    d_proj = product_tn(attended, grad_branch)
    soft_probs = attend(qkv_bf[:, :model_width], key_values, doc_mask)
    seq_len = key_values.shape[0]
    queries = qkv_bf[:, :model_width].reshape(-1, HEADS, HEAD_DIM)
    key_heads = key_values[:, :model_width].reshape(seq_len, HEADS, HEAD_DIM)
    value_heads = key_values[:, model_width:].reshape(seq_len, HEADS, HEAD_DIM)
    grad_heads = grad_att.reshape(-1, HEADS, HEAD_DIM)
    grad_prob = jnp.einsum("qhd,khd->hqk", grad_heads, value_heads, preferred_element_type=F32)
    grad_score = soft_probs * (grad_prob - jnp.sum(soft_probs * grad_prob, axis=-1, keepdims=True))
    grad_score = grad_score.astype(BF)
    grad_query = (
        jnp.einsum("hqk,khd->qhd", grad_score, key_heads, preferred_element_type=F32).reshape(
            -1, model_width
        )
        * 0.125
    )
    grad_keys = (
        jnp.einsum("hqk,qhd->khd", grad_score, queries, preferred_element_type=F32).reshape(
            seq_len, model_width
        )
        * 0.125
    )
    grad_values = jnp.einsum(
        "hqk,qhd->khd", soft_probs.astype(BF), grad_heads, preferred_element_type=F32
    ).reshape(seq_len, model_width)
    if earlier is not None:
        grad_query, first_earlier = lax.optimization_barrier((grad_query, first_earlier))
    grad_pairs = jnp.concatenate([grad_keys, grad_values], axis=1)
    own, core, far, both = jnp.split(grad_pairs, 4, axis=0)
    far = far + swap(both, "c")
    own = own + swap(core, "c")
    grad_pairs = own + wide(z_flip(far.astype(BF)))
    grad_mixed = jnp.concatenate([grad_query, grad_pairs], axis=1).astype(BF)
    late = product_tn(normed, grad_mixed), d_proj
    _, norm_back_a = jax.vjp(layer_norm, residual, gain_a, shift_a)
    mixed_sums = jnp.sum(wide(grad_mixed), axis=0)
    grad_resid, g_gain_a, g_shift_a = norm_back_a(product_nt(grad_mixed, w_qkv))
    grad_resid = grad_resid + grad_mid
    grad_resid, late = lax.optimization_barrier((grad_resid, late))
    if earlier is not None:
        late, second_earlier, grad_resid = lax.optimization_barrier((late, earlier[1], grad_resid))
        earlier = first_earlier, second_earlier
    late = lax.psum(late, ("dp", "seq"))
    bias_rows = jnp.concatenate(
        [
            jnp.stack([mixed_sums[:model_width], mixed_sums[2 * model_width :], b_proj]),
            b_fc.reshape(-1, model_width),
            b_out[None],
        ],
        axis=0,
    )
    return (
        grad_resid,
        (early, late),
        earlier,
        (g_gain_a, g_gain_b, g_shift_a, g_shift_b, bias_rows),
    )


def adam_update(param, grad, first, second, rate, decay):
    first = first_decay * first + (1.0 - first_decay) * grad
    second = second_decay * second + (1.0 - second_decay) * grad * grad
    fixed_first = first / (1.0 - first_decay**STEP)
    fixed_second = second / (1.0 - second_decay**STEP)
    return (
        param - rate * (fixed_first / (jnp.sqrt(fixed_second) + adam_epsilon) + decay * param),
        first,
        second,
    )


def squared_blocks(flat):
    return flat.reshape(-1, BS, BS)


def shards(
    token_ids,
    doc_ids,
    pick_slots,
    labels,
    vocab_table,
    vocab_first,
    vocab_second,
    positions,
    positions_first,
    positions_second,
    small_params,
    small_first,
    small_second,
    weights,
    stat_left,
    stat_right,
    root_left,
    root_right,
    anchor,
    fisher,
    owners,
):
    row_at = lax.axis_index("dp")
    seq_at = lax.axis_index("seq")
    z_hi, core = seq_at // 2, seq_at % 2
    y_at, zl_at, x_at = row_at // 8, (row_at // 4) % 2, row_at % 4
    span_len = token_ids.shape[1]
    model_width = small_params.shape[1]
    half_width = model_width // 2
    table_rows = vocab_table.shape[0]
    padded = -(-table_rows // 64) * 64
    vocab_start = row_at * 2 * table_rows
    own_shift = jnp.where(core == 0, jnp.array([0, 1, 2, 3]), jnp.array([0, 3, 2, 1]))

    own_slots = (core * 32 + row_at) * 3 + jnp.arange(3)
    own_tiles = jnp.take(
        jnp.where(z_hi == 0, owners[0], owners[1]), own_slots, axis=0
    )
    own_places = tile_places(own_tiles)

    own_weights = jnp.pad(squared_blocks(weights), ((0, 0), (0, 0), (0, 2 * LANES - BS)))
    layer_weights = []
    for layer_idx in range(LAYERS):
        here = jnp.where(z_hi == layer_idx, own_places[0], -1)
        matrices = spread_tiles(own_places.at[0].set(here), own_weights.astype(BF).astype(F32))
        if layer_idx:
            matrices, layer_weights[-1] = lax.optimization_barrier((matrices, layer_weights[-1]))
        layer_weights.append(lax.psum(matrices, ("seq", "dp")))

    sequences = token_ids.shape[0]
    shard_of = token_ids // (2 * table_rows)
    held_by = (shard_of[:, None, :] == jnp.arange(sequences)[None, :, None]).astype(BF)
    before = (jnp.arange(span_len)[:, None] <= jnp.arange(span_len)[None, :]).astype(BF)
    ranks = product(held_by.reshape(-1, span_len), before).reshape(held_by.shape).astype(jnp.int32) - 1
    crowds = jnp.sum((ranks[:, :, -1] >= SLOTS).astype(F32))
    counts = jnp.stack([crowds, jnp.sum((pick_slots >= 0).astype(F32))])
    counts = jnp.broadcast_to(counts[:, None], (2, LANES))

    own_part = jnp.pad(vocab_table.astype(BF), ((0, padded - table_rows), (0, 0)))
    near_part, far_part = swap(own_part, "c"), z_flip(own_part)
    counts = counts + swap(counts, "c")
    counts = counts + swap(counts, "zh")
    crowded, pick_count = counts[0, 0] > 0.0, counts[1, 0]
    both_parts = jnp.stack([own_part, far_part])
    near_parts = jnp.stack([near_part, swap(far_part, "c")])
    table_bf = jnp.where(
        core == 0,
        jnp.concatenate([both_parts, near_parts], axis=2),
        jnp.concatenate([near_parts, both_parts], axis=2),
    ).reshape(2 * padded, model_width)
    vocab_rows = 2 * padded
    row_used = jnp.arange(vocab_rows) % padded < table_rows

    def local_row(ids):
        offset = ids - vocab_start
        inside = (offset >= 0) & (offset < 2 * table_rows)
        return jnp.where(inside, ((offset % 2) ^ z_hi) * padded + offset // 2, -1)

    all_params = [layer_params(small_params, layer_idx) for layer_idx in range(LAYERS)]

    all_rows = local_row(token_ids)
    own_ranks = lax.dynamic_index_in_dim(ranks, row_at, 1, keepdims=False)
    slots = jnp.arange(SLOTS)
    in_slot = (own_ranks[:, None, :] == slots[None, :, None]) & (all_rows >= 0)[:, None, :]
    slot_rows = jnp.sum(jnp.where(in_slot, all_rows[:, None, :] + 1, 0), axis=2) - 1
    arrived = exchanged(pick_table_rows(slot_rows, table_bf), "dp")
    my_shards = lax.dynamic_index_in_dim(shard_of, row_at, 0, keepdims=False)
    my_ranks = lax.dynamic_index_in_dim(ranks, row_at, 0, keepdims=False)
    my_rank = jnp.sum(jnp.where(my_shards[None, :] == jnp.arange(sequences)[:, None], my_ranks, 0), axis=0)
    my_slots = jnp.where(my_rank < SLOTS, my_shards * SLOTS + my_rank, -1)
    slot_hot = my_slots[:, None] == jnp.arange(sequences * SLOTS)[None, :]
    looked = product(slot_hot.astype(BF), arrived)

    far_y = (y_at + own_shift) % 4
    far_x = (x_at + own_shift) % 4
    far_z = zl_at ^ jnp.arange(2)
    rows_xyz = far_y[None, :, None] * 8 + far_z[None, None, :] * 4 + far_x[:, None, None]
    crowd_rows = jnp.where(own_ranks >= SLOTS, all_rows, -1)
    crowd_rows = jnp.take(crowd_rows, rows_xyz.reshape(-1), axis=0)

    def quarters(value):
        return jnp.split(value, 4, axis=0)

    def dense_rows():
        spread_ids = jnp.broadcast_to(crowd_rows.reshape(-1, 1), (crowd_rows.size, LANES))
        found0, found1, found2, found3 = lookup(spread_ids, table_bf)

        def plain_reduce4(parts, axis):
            near = turn(parts[1] + turn(parts[2], axis, 1), axis, 1)
            return (parts[0] + near) + turn(parts[3], axis, -1)

        def last_pair(value):
            return value[:span_len] + swap(value[span_len:], "zl")

        parts = [
            last_pair(plain_reduce4(quarters(plain_reduce4(quarters(found0), "x")), "y")),
            last_pair(plain_reduce4(quarters(plain_reduce4(quarters(found1), "y")), "x")),
            plain_reduce4(quarters(plain_reduce4(quarters(found2 + swap(found3, "zl")), "x")), "y"),
        ]
        return wide(jnp.concatenate(parts, axis=1))

    looked = looked + lax.cond(crowded, dense_rows, lambda: jnp.zeros((span_len, model_width), F32))
    residual = looked + positions

    doc_row = doc_ids[0]
    query_places = seq_at * span_len + jnp.arange(span_len)
    own_docs = lax.dynamic_slice_in_dim(doc_row, seq_at * span_len, span_len)
    part_order = seq_at ^ jnp.arange(4)
    key_places = (part_order[:, None] * span_len + jnp.arange(span_len)[None]).reshape(-1)
    key_docs = jnp.take(doc_row.reshape(4, span_len), part_order, axis=0).reshape(-1)
    doc_mask = (query_places[:, None] >= key_places[None, :]) & (
        own_docs[:, None] == key_docs[None, :]
    )
    kept_layers = []
    for layer_idx in range(LAYERS):
        residual, kept_values = layer_forward(
            residual, layer_weights[layer_idx], all_params[layer_idx], doc_mask
        )
        kept_layers.append(kept_values)
    gain_rows = 2 * LAYERS + 1
    final_norm, final_back = jax.vjp(
        layer_norm, residual, small_params[2 * LAYERS], small_params[gain_rows + 2 * LAYERS]
    )
    final_bf = final_norm.astype(BF)

    pick_dev = pick_slots.shape[1]
    own_picks = lax.dynamic_index_in_dim(pick_slots, row_at, 0, keepdims=False)
    own_valid = own_picks >= 0
    pick_rows = jnp.maximum(own_picks, 0)
    chosen = jnp.where(own_valid[:, None], jnp.take(final_bf, pick_rows, axis=0), jnp.zeros((), BF))
    gathered = exchanged(jnp.tile(chosen, (sequences, 1)), "dp")
    valid_all = pick_slots.reshape(-1) >= 0
    label_rows = local_row(labels.reshape(-1))
    logits = jnp.where(row_used[None, :], product_nt(gathered, table_bf), -1e30)
    hits = label_rows[:, None] == jnp.arange(vocab_rows)[None, :]
    peak = jnp.max(logits, axis=1)
    exp_total = jnp.sum(jnp.exp(logits - peak[:, None]), axis=1)
    target = jnp.sum(jnp.where(hits, logits, 0.0), axis=1)
    stats = jnp.stack([peak, exp_total, target]).reshape(1, -1)
    stats = exchanged(jnp.tile(stats, (sequences, 1)), "dp").reshape(sequences, 3, -1)
    top = jnp.max(stats[:, 0], axis=0)
    log_total = top + jnp.log(jnp.sum(stats[:, 1] * jnp.exp(stats[:, 0] - top[None]), axis=0))
    losses = jnp.where(valid_all, log_total - jnp.sum(stats[:, 2], axis=0), 0.0)
    loss_own = jnp.sum(lax.dynamic_slice_in_dim(losses, row_at * pick_dev, pick_dev))
    grad_logits = jnp.where(
        valid_all[:, None], jnp.exp(logits - log_total[:, None]) - hits.astype(F32), 0.0
    ).astype(BF)
    head_grad = product_tn(grad_logits, gathered)
    grad_chosen = exchanged(product(grad_logits, table_bf).astype(BF), "dp")
    grad_chosen = jnp.sum(wide(grad_chosen.reshape(sequences, pick_dev, model_width)), axis=0)
    grad_final = (
        jnp.zeros((span_len, model_width), F32)
        .at[pick_rows]
        .add(jnp.where(own_valid[:, None], grad_chosen, 0.0))
    )
    grad_resid, g_final_gain, g_final_shift = final_back(grad_final)

    summed = None
    layer_grads = []
    small_parts = [None] * LAYERS
    for layer_idx in reversed(range(LAYERS)):
        grad_resid, matrix_grads, earlier, small_parts[layer_idx] = layer_backward(
            grad_resid,
            kept_layers[layer_idx],
            layer_weights[layer_idx],
            all_params[layer_idx],
            doc_mask,
            summed,
        )
        if earlier is not None:
            layer_grads.append(earlier)
        summed = matrix_grads
    layer_grads.append(summed)

    gain_list = []
    shift_list = []
    for layer_idx in range(LAYERS):
        gain_list += [small_parts[layer_idx][0], small_parts[layer_idx][1]]
        shift_list += [small_parts[layer_idx][2], small_parts[layer_idx][3]]
    first_term = loss_own.astype(BF)
    second_term = (loss_own - wide(first_term)).astype(BF)
    third_term = (loss_own - wide(first_term) - wide(second_term)).astype(BF)
    scalars = jnp.stack([wide(first_term), wide(second_term), wide(third_term)])
    small_grad = jnp.concatenate(
        [jnp.stack(gain_list + [g_final_gain]), jnp.stack(shift_list + [g_final_shift])]
        + [small_parts[layer_idx][4] for layer_idx in range(LAYERS)]
        + [jnp.pad(scalars, (0, model_width - 3))[None]],
        axis=0,
    )
    small_grad = jnp.pad(small_grad, ((0, sequences - small_grad.shape[0]), (0, 0)))

    grad_bf = grad_resid.astype(BF)
    slot_grads = product_tn(slot_hot.astype(BF), grad_bf).astype(BF)
    own_rows = span_len // sequences
    spare = 16 - own_rows - 1
    outgoing = jnp.concatenate(
        [
            slot_grads.reshape(sequences, SLOTS, model_width),
            grad_bf.reshape(sequences, own_rows, model_width),
            small_grad.astype(BF)[:, None],
            jnp.zeros((sequences, spare, model_width), BF),
        ],
        axis=1,
    )
    arrived = exchanged(outgoing.reshape(-1, model_width), "dp").reshape(sequences, -1, model_width)
    pos_own = jnp.sum(wide(arrived[:, SLOTS : SLOTS + own_rows]), axis=0)
    small_own = jnp.sum(wide(arrived[:, SLOTS + own_rows]), axis=0)
    small_own = jnp.broadcast_to(small_own[None], (8, model_width))
    grad_table = add_table_rows(
        slot_rows, head_grad, arrived[:, :SLOTS].reshape(-1, model_width)
    )

    def dense_grads():
        columns = [grad_bf[:, at : at + 256] for at in range(0, model_width, 256)]

        pair0 = joined(columns[0], swap(columns[0], "zl"))
        spread0 = joined(*gather4(joined(*gather4(pair0, "y")), "x"))
        pair1 = joined(columns[1], swap(columns[1], "zl"))
        spread1 = joined(*gather4(joined(*gather4(pair1, "x")), "y"))
        spread2 = joined(*gather4(joined(*gather4(columns[2], "y")), "x"))
        spread3 = swap(spread2, "zl")
        return scatter_rows(
            crowd_rows.reshape(16, 1, 512), grad_table, (spread0, spread1, spread2, spread3)
        )

    grad_table = lax.cond(crowded, dense_grads, lambda: grad_table)
    left_half, right_half = grad_table[:, :half_width], grad_table[:, half_width:]
    mine = jnp.where(core == 0, left_half, right_half)
    theirs = jnp.where(core == 0, right_half, left_half)
    grad_half = mine + swap(theirs, "c")
    small_own = small_own + swap(small_own, "c")
    small_own = (small_own + swap(small_own, "zh"))[0]
    far_grad = z_flip(grad_half[padded : padded + table_rows].astype(BF))
    grad_own = grad_half[:table_rows] + wide(far_grad)
    grad_places = own_places.at[0].add(z_hi * len(MATRICES))
    own_blocks = cut_tiles(
        grad_places, [value for early, late in layer_grads[::-1] for value in (*late, *early)]
    )
    shared = joined(pos_own, jnp.pad(small_own[None], ((0, 7), (0, 0))))
    shared = exchanged(jnp.tile(shared, (sequences, 1)), "dp").reshape(sequences, -1, model_width)

    g_table = grad_own / pick_count
    g_ce = own_blocks.reshape(weights.shape) / pick_count
    g_blocks = g_ce + ewc_weight * fisher * (weights - anchor)
    g_pos_own = pos_own / pick_count
    local_squares = jnp.sum(g_table * g_table) + jnp.sum(g_blocks * g_blocks)
    local_squares = local_squares + jnp.sum(g_pos_own * g_pos_own)
    g_small_own = small_own / pick_count
    local_squares = local_squares + jnp.where(
        (row_at < small_params.shape[0]) & (seq_at == 0), jnp.sum(g_small_own * g_small_own), 0.0
    )
    all_squares = exchanged(jnp.broadcast_to(local_squares, (len(COORDS), LANES)), ("seq", "dp"))

    def products(grad, root_l, root_r):
        return exact_mm(grad, grad.T), exact_mm(grad.T, grad), exact_mm(exact_mm(root_l, grad), root_r)

    block_products = jax.vmap(products)(
        squared_blocks(g_blocks), squared_blocks(root_left), squared_blocks(root_right)
    )
    left_mm, right_mm, direction = (value.reshape(weights.shape) for value in block_products)
    all_squares, shared, left_mm, right_mm, direction = lax.optimization_barrier(
        (all_squares, shared, left_mm, right_mm, direction)
    )
    pos_sum = shared[:, :own_rows].reshape(span_len, model_width)
    small_all = shared[:, own_rows]
    rows = small_params.shape[0]
    ce_sum = jnp.sum(small_all[rows, :3])
    g_pos = pos_sum / pick_count
    g_small = small_all[:rows] / pick_count
    grad_norm = jnp.sqrt(jnp.sum(all_squares[:, 0]))
    factor = jnp.minimum(1.0, clip_bound / grad_norm)
    table_new, table_first, table_second = adam_update(
        vocab_table, factor * g_table, vocab_first, vocab_second, table_rate, decay_rate
    )
    pos_new, pos_first, pos_second = adam_update(
        positions, factor * g_pos, positions_first, positions_second, table_rate, 0.0
    )
    small_new, small_first_new, small_second_new = adam_update(
        small_params, factor * g_small, small_first, small_second, small_rate, 0.0
    )
    block_grad = factor * g_blocks

    direction = factor * direction
    mean_square = jnp.mean(direction * direction, axis=1, keepdims=True)
    direction = direction * lax.rsqrt(mean_square + graft_epsilon)
    weights_new = weights - shampoo_rate * (direction + decay_rate * weights)
    square = factor * factor
    left_new = stat_decay * stat_left + (1.0 - stat_decay) * (square * left_mm)
    right_new = stat_decay * stat_right + (1.0 - stat_decay) * (square * right_mm)
    fisher_new = fisher_decay * fisher + (1.0 - fisher_decay) * g_ce * g_ce
    return (
        ce_sum,
        pick_count,
        grad_norm,
        table_new,
        table_first,
        table_second,
        pos_new,
        pos_first,
        pos_second,
        small_new,
        small_first_new,
        small_second_new,
        weights_new,
        left_new,
        right_new,
        block_grad,
        fisher_new,
    )


def solution(mesh):
    split = P(("seq", "dp"), None)
    table = P("dp", "seq")
    in_specs = (
        (P(None, "seq"), P("dp", None), P(None, "seq"), P(None, "seq"))
        + (table,) * 3
        + (P("seq", None),) * 3
        + (P(),) * 3
        + (split,) * 7
        + (P(),)
    )
    out_specs = (
        (P(),) * 3 + (table,) * 3 + (P("seq", None),) * 3 + (P(),) * 3 + (split,) * 5
    )
    return jax.shard_map(shards, mesh=mesh, in_specs=in_specs, out_specs=out_specs, check_vma=False)
```
